512 devices in a mesh: req: 128 (over y, z, core), mp: 4 (over x).
Axes of the slice: x: 4, y: 8, z: 8, core: 2. Of those that a mesh axis runs over, the one named last changes fastest.
Arguments:
- cand_feats: bfloat16 [65536, 1024], P('req', 'mp'), may hold values from -6 to 6
- cand_perm: int32 [128, 512], P('req'), may hold values from 0 to 511, each once within a row
- w_in: bfloat16 [1024, 4, 1024], P(None, None, 'mp'), may hold values from -0.1875 to 0.1875
- w_out: bfloat16 [1024, 1024], P('mp'), may hold values from -0.1875 to 0.1875
- cache_k: bfloat16 [4096, 32, 1024], P('req', None, 'mp'), may hold values from -6 to 6
- cache_v: bfloat16 [4096, 32, 1024], P('req', None, 'mp'), may hold values from -1.5 to 1.5
- hist_len: int32 [128], P('req'), may hold values from 1 to 4096, as said below
- hist_home: int32 [128], replicated, may hold values from 0 to 127
- hist_slot: int32 [128, 128], replicated, may hold values from 0 to 31
- hist_mask: int32 [128, 4, 128], P('req'), may hold values 0 or 1
Outputs:
- scored: bfloat16 [65536, 1024], P('req', 'mp')
The draws below stay inside these ranges and needn't reach their ends.
Inputs may be any that keep to these rules, and one draw needn't show every extreme that they name: `cand_perm`: each row is a permutation of 0 to 511. `hist_len`: some request has a history of 4096 events.
All inputs are finite; a program needn't handle non-finite values. No bound on the sum of `hist_mask` on one device may be relied on, other than what follows from the above.
Results may differ from the reference program's by a relative error of at most 0.0067.
Values may be sent and summed in bfloat16 or wider, within the bound.
No kernel may reach another device: no remote copies, remote signals or barrier semaphores. Data moves between devices by JAX's collectives and lax.ppermute only.
A program may use at most 64 MiB of HBM per device.

```python
import jax
import jax.numpy as jnp
from jax import lax

D = 1024
HEADS = 8
DH = 128
CANDS = 512
BLK = 32
MAXBLK = 128
BLK_DEV = 32
GROUP = 128
REQS = 128
CSLOT = 4
CGRP = 4
N_REQ = 128


def draw_hist_len(key, part):
    key = jax.random.fold_in(key, 11)
    first_key, second_key = jax.random.split(key)
    lengths = jax.random.randint(first_key, (REQS,), 1, MAXBLK * BLK + 1)
    chosen = jax.random.randint(second_key, (), 0, REQS)
    return jnp.where(jnp.arange(REQS) == chosen, MAXBLK * BLK, lengths).astype(jnp.int32)


def place_ends(entries, key, low, top_value):
    extent = entries.shape
    spot = [jax.random.randint(jax.random.fold_in(key, axis), (), 0, extent[axis]) for axis in range(len(extent))]
    entries = entries.at[tuple(spot)].set(low)
    longest = extent.index(max(extent))
    spot[longest] = (spot[longest] + 1) % extent[longest]
    return entries.at[tuple(spot)].set(top_value)


def shard_levels(stream_key, shape, pieces, low, largest):
    gain, own = 1.0, jax.random.fold_in(stream_key, 6)
    for axis_at, blocks in pieces:
        heights = jnp.exp(jax.random.uniform(jax.random.fold_in(own, axis_at), (blocks,), jnp.float32, low / len(pieces), largest / len(pieces)))
        gain = gain * jnp.repeat(heights, shape[axis_at] // blocks).reshape([-1 if axis == axis_at else 1 for axis in range(len(shape))])
    return gain


def noise(stream_key, dims, scale, most, cuts=(), kind=jnp.bfloat16):
    drawn = jax.random.normal(stream_key, dims, jnp.float32) * scale
    if len(cuts) > 0:
        drawn = shard_levels(stream_key, dims, cuts, -0.22, 0.18) * drawn
    return jnp.clip(drawn, min=-most, max=most).astype(kind)


def setup_inputs(seed: int = 0) -> dict:
    keys = jax.random.split(jax.random.key(seed), 11)
    return {
        "cand_feats": noise(keys[0], (N_REQ * N_REQ * CSLOT, D), 1.0, 6.0, ((0, 128), (1, 4))),
        "cand_perm": jax.vmap(lambda own: jax.random.permutation(own, CANDS))(jax.random.split(keys[1], REQS)).reshape((REQS, CANDS)).astype(jnp.int32),
        "w_in": noise(keys[2], (D, 4, HEADS * DH), D ** -0.5, 0.1875, ((2, 4),)),
        "w_out": noise(keys[3], (HEADS * DH, D), (HEADS * DH) ** -0.5, 0.1875, ((0, 4),)),
        "cache_k": noise(keys[4], (N_REQ * BLK_DEV, BLK, HEADS * DH), 1.0, 6.0, ((0, 128), (2, 4))),
        "cache_v": noise(keys[5], (N_REQ * BLK_DEV, BLK, HEADS * DH), 0.25, 1.5, ((0, 128), (2, 4))),
        "hist_len": draw_hist_len(jax.random.fold_in(keys[10], 71), 0),
        "hist_home": place_ends(jax.random.randint(keys[7], (REQS,), 0, N_REQ), jax.random.fold_in(keys[7], 1), 0, N_REQ - 1).astype(jnp.int32),
        "hist_slot": place_ends(jax.random.randint(keys[8], (REQS, MAXBLK), 0, BLK_DEV), jax.random.fold_in(keys[8], 1), 0, BLK_DEV - 1).astype(jnp.int32),
        "hist_mask": place_ends((jax.random.randint(keys[9], (REQS, CGRP, MAXBLK), 0, 4) < 3).astype(jnp.int32), jax.random.fold_in(keys[9], 1), 0, 1),
    }


EPS = 1e-05

def reference(cand_feats, cand_perm, w_in, w_out, cache_k, cache_v, hist_len, hist_home, hist_slot, hist_mask):
    cand_slot = CANDS // N_REQ
    key_count = MAXBLK * BLK
    width_all = HEADS * DH
    score_scale = DH ** (-0.5)
    w_flat = w_in.reshape(D, 4 * width_all)

    def per_request(request):
        position = cand_perm[request]
        row_index = position // cand_slot * (N_REQ * cand_slot) + request * cand_slot + position % cand_slot
        features = cand_feats[row_index].astype(jnp.float32)
        centred = features - lax.optimization_barrier(jnp.mean(features, axis=1, keepdims=True))
        spread = lax.optimization_barrier(jnp.mean(centred * centred, axis=1, keepdims=True))
        normed = (centred * lax.rsqrt(spread + EPS)).astype(jnp.bfloat16)
        parts = jax.nn.silu(jnp.dot(normed, w_flat, preferred_element_type=jnp.float32)).astype(jnp.bfloat16)
        parts = parts.reshape(CANDS, 4, width_all)
        gate_u, value_v, query_q, key_k = (parts[:, 0], parts[:, 1], parts[:, 2], parts[:, 3])
        block_order = jnp.arange(MAXBLK, dtype=jnp.int32)
        source = (hist_home[request] + block_order) % N_REQ
        blocks = (source * BLK_DEV + hist_slot[request]).astype(jnp.int32)
        hist_keys = cache_k[blocks].reshape(key_count, width_all)
        hist_values = cache_v[blocks].reshape(key_count, width_all)
        live_keys = (jnp.arange(key_count, dtype=jnp.int32) < hist_len[request]).astype(jnp.float32)
        block_mask = jnp.repeat(hist_mask[request].astype(jnp.float32), BLK, axis=1) * live_keys[None, :]
        outputs = []
        for head_index in range(HEADS):
            lo_col = head_index * DH
            q_head = query_q[:, lo_col:lo_col + DH]
            scores = jnp.dot(q_head, hist_keys[:, lo_col:lo_col + DH].T, preferred_element_type=jnp.float32) * score_scale
            weights = jax.nn.silu(scores).reshape(CANDS // GROUP, GROUP, key_count) * block_mask[:, None, :]
            weights = weights.reshape(CANDS, key_count).astype(jnp.bfloat16)
            own_score = lax.optimization_barrier(jnp.sum(q_head.astype(jnp.float32) * key_k[:, lo_col:lo_col + DH].astype(jnp.float32), axis=1, keepdims=True)) * score_scale
            own_term = jax.nn.silu(own_score) * value_v[:, lo_col:lo_col + DH].astype(jnp.float32)
            outputs.append(jnp.dot(weights, hist_values[:, lo_col:lo_col + DH], preferred_element_type=jnp.float32) + own_term)
        attn = jnp.concatenate(outputs, axis=1)
        attn_centred = attn - lax.optimization_barrier(jnp.mean(attn, axis=1, keepdims=True))
        attn_spread = lax.optimization_barrier(jnp.mean(attn_centred * attn_centred, axis=1, keepdims=True))
        hidden = (attn_centred * lax.rsqrt(attn_spread + EPS) * gate_u.astype(jnp.float32)).astype(jnp.bfloat16)
        mixed = jnp.dot(hidden, w_out, preferred_element_type=jnp.float32)
        return (features + mixed).astype(jnp.bfloat16)
    scored = lax.map(per_request, jnp.arange(N_REQ, dtype=jnp.int32))
    return scored.reshape(N_REQ * CANDS, D)
```

```python
import functools

import jax
import jax.numpy as jnp
from jax import lax
from jax.experimental import pallas as pl
from jax.experimental.pallas import tpu as pltpu
from jax.sharding import PartitionSpec as P

HEADS = 8
DH = 128
BLK = 32
MAXBLK = 128
GROUP = 128
EPS = 1e-05
VMEM = 48 * 1024 * 1024


def cost(flops, nbytes, trans=0):
    return pl.CostEstimate(flops=flops, bytes_accessed=nbytes, transcendentals=trans)


def pack_kernel(slots, cache, *refs):
    extra, out = (refs[0], refs[1]) if len(refs) == 2 else (None, refs[0])
    per = out.shape[0]
    base = pl.program_id(0) * per
    for i in range(per):
        slot = slots[base + i]
        block = cache[slot]
        out[i, :BLK, :] = block[:, :DH]
        out[i, BLK : 2 * BLK, :] = block[:, DH:]
    if extra is not None:
        out[:, 2 * BLK :, :] = extra[...]


def pack(slots, cache, extra=None):
    shards = slots.shape[0]
    per = 16
    rows = 2 * BLK + (0 if extra is None else extra.shape[1])
    in_specs = [pl.BlockSpec(cache.shape, lambda i, s: (0, 0, 0))]
    args = [cache]
    if extra is not None:
        in_specs.append(pl.BlockSpec((per, extra.shape[1], DH), lambda i, s: (i, 0, 0)))
        args.append(extra)
    return pl.pallas_call(
        pack_kernel,
        out_shape=jax.ShapeDtypeStruct((shards, rows, DH), cache.dtype),
        grid_spec=pltpu.PrefetchScalarGridSpec(
            num_scalar_prefetch=1,
            grid=(shards // per,),
            in_specs=in_specs,
            out_specs=pl.BlockSpec((per, rows, DH), lambda i, s: (i, 0, 0)),
        ),
        compiler_params=pltpu.CompilerParams(vmem_limit_bytes=VMEM),
        cost_estimate=cost(0, 2 * shards * rows * DH * 2),
        name="pack",
    )(slots, *args)


def project_kernel(rows, w, gate, query, own):
    features = rows[...].astype(jnp.float32)
    centred = features - jnp.mean(features, axis=1, keepdims=True)
    spread = jnp.mean(centred * centred, axis=1, keepdims=True)
    normed = (centred * lax.rsqrt(spread + EPS)).astype(jnp.bfloat16)
    width = gate.shape[1]

    def part(i):
        x = jnp.dot(
            normed, w[:, i * width : (i + 1) * width], preferred_element_type=jnp.float32
        )
        half = 0.5 * x
        return (half + half * jnp.tanh(half)).astype(jnp.bfloat16)

    gate[...] = part(0)
    value = part(1).astype(jnp.float32)
    q = part(2)
    query[...] = q
    key = part(3).astype(jnp.float32)
    product = q.astype(jnp.float32) * key
    for h in range(width // DH):
        cols = slice(h * DH, (h + 1) * DH)
        half = jnp.sum(product[:, cols], axis=1, keepdims=True) * (0.5 * DH**-0.5)
        own[:, cols] = (half + half * jnp.tanh(half)) * value[:, cols]


def project(rows, w, width):
    cands, depth = rows.shape
    step = 128
    block = lambda n: pl.BlockSpec((step, n), lambda i: (i, 0))
    return pl.pallas_call(
        project_kernel,
        out_shape=(
            jax.ShapeDtypeStruct((cands, width), jnp.bfloat16),
            jax.ShapeDtypeStruct((cands, width), jnp.bfloat16),
            jax.ShapeDtypeStruct((cands, width), jnp.float32),
        ),
        grid=(cands // step,),
        in_specs=[block(depth), pl.BlockSpec(w.shape, lambda i: (0, 0))],
        out_specs=(block(width), block(width), block(width)),
        compiler_params=pltpu.CompilerParams(vmem_limit_bytes=VMEM),
        cost_estimate=cost(2 * cands * depth * 4 * width, 6 << 20, cands * 4 * width),
        name="project",
    )(rows, w)


def weights_kernel(query, keys, mask, out):
    sources = keys.shape[0]
    n = sources * BLK
    for h in range(query.shape[1] // DH):
        k = keys[:, h * BLK : (h + 1) * BLK, :].reshape(n, DH)
        for g in range(query.shape[0] // GROUP):
            rows = slice(g * GROUP, (g + 1) * GROUP)
            s = lax.dot_general(
                query[rows, h * DH : (h + 1) * DH],
                k,
                (((1,), (1,)), ((), ())),
                preferred_element_type=jnp.float32,
            )
            half = s * mask[g : g + 1, :]
            out[h, rows, :] = (half + half * jnp.tanh(half)).astype(jnp.bfloat16)


def attention_weights(query, got, mask):
    shards = got.shape[0]
    cands, width = query.shape
    heads = width // DH
    per = 16
    return pl.pallas_call(
        weights_kernel,
        out_shape=jax.ShapeDtypeStruct((heads, cands, shards * BLK), jnp.bfloat16),
        grid=(shards // per,),
        in_specs=[
            pl.BlockSpec((cands, width), lambda i: (0, 0)),
            pl.BlockSpec((per, 2 * BLK, DH), lambda i: (i, 0, 0)),
            pl.BlockSpec((mask.shape[0], per * BLK), lambda i: (0, i)),
        ],
        out_specs=pl.BlockSpec((heads, cands, per * BLK), lambda i: (0, 0, i)),
        compiler_params=pltpu.CompilerParams(vmem_limit_bytes=VMEM),
        cost_estimate=cost(
            2 * cands * shards * BLK * width, 12 << 20, heads * cands * shards * BLK
        ),
        name="weights",
    )(query, got, mask)


def values_kernel(weights, values, own, out, total):
    step = pl.program_id(0)
    n = values.shape[0] * BLK

    @pl.when(step == 0)
    def _():
        total[...] = own[...]

    for h in range(weights.shape[0]):
        v = values[:, h * BLK : (h + 1) * BLK, :].reshape(n, DH)
        total[:, h * DH : (h + 1) * DH] += jnp.dot(
            weights[h], v, preferred_element_type=jnp.float32
        )

    @pl.when(step == pl.num_programs(0) - 1)
    def _():
        done = total[...].astype(jnp.bfloat16)
        for i in range(out.shape[0]):
            out[i] = done


def weighted_values(weights, got, own, copies):
    shards = got.shape[0]
    heads, cands, _ = weights.shape
    width = own.shape[1]
    per = 16
    return pl.pallas_call(
        values_kernel,
        out_shape=jax.ShapeDtypeStruct((copies, cands, width), jnp.bfloat16),
        grid=(shards // per,),
        in_specs=[
            pl.BlockSpec((heads, cands, per * BLK), lambda i: (0, 0, i)),
            pl.BlockSpec((per, 2 * BLK, DH), lambda i: (i, 0, 0)),
            pl.BlockSpec((cands, width), lambda i: (0, 0)),
        ],
        out_specs=pl.BlockSpec((copies, cands, width), lambda i: (0, 0, 0)),
        scratch_shapes=[pltpu.VMEM((cands, width), jnp.float32)],
        compiler_params=pltpu.CompilerParams(vmem_limit_bytes=VMEM),
        cost_estimate=cost(2 * cands * shards * BLK * width, 12 << 20),
        name="values",
    )(weights, got, own)


def finish_kernel(attn, gate, w, rows, out):
    parts, _, width = attn.shape
    pieces = [attn[i].astype(jnp.float32) for i in range(parts)]
    total = parts * width
    mean = sum(jnp.sum(p, axis=1, keepdims=True) for p in pieces) / total
    centred = [p - mean for p in pieces]
    spread = sum(jnp.sum(c * c, axis=1, keepdims=True) for c in centred) / total
    scale = lax.rsqrt(spread + EPS)
    result = rows[...].astype(jnp.float32)
    for i in range(parts):
        hidden = (centred[i] * scale * gate[i].astype(jnp.float32)).astype(jnp.bfloat16)
        result += jnp.dot(
            hidden, w[i * width : (i + 1) * width, :], preferred_element_type=jnp.float32
        )
    out[...] = result.astype(out.dtype)


def finish(attn, gate, w, rows):
    parts, cands, width = attn.shape
    step = 128
    stack = pl.BlockSpec((parts, step, width), lambda i: (0, i, 0))
    flat = pl.BlockSpec((step, rows.shape[1]), lambda i: (i, 0))
    return pl.pallas_call(
        finish_kernel,
        out_shape=jax.ShapeDtypeStruct(rows.shape, jnp.bfloat16),
        grid=(cands // step,),
        in_specs=[stack, stack, pl.BlockSpec(w.shape, lambda i: (0, 0)), flat],
        out_specs=flat,
        compiler_params=pltpu.CompilerParams(vmem_limit_bytes=VMEM),
        cost_estimate=cost(2 * cands * parts * width * rows.shape[1], 3 << 20),
        name="finish",
    )(attn, gate, w, rows)


def local(
    cand_feats, cand_perm, w_in, w_out, cache_k, cache_v, hist_len, hist_home, hist_slot, hist_mask
):
    shards = lax.axis_size("req")
    split = lax.axis_size("mp")
    me = lax.axis_index("req")
    part = lax.axis_index("mp")
    columns = cand_feats.shape[1]
    cand_slot = cand_feats.shape[0] // shards
    cands = cand_perm.shape[1]
    width = w_in.shape[2]

    wanted = (me - hist_home) % shards
    places = jnp.arange(MAXBLK, dtype=jnp.int32)
    slots = jnp.sum(jnp.where(places[None, :] == wanted[:, None], hist_slot, 0), axis=1)

    halves = columns // DH
    cand_rows = (
        cand_feats.reshape(shards, cand_slot, halves, DH)
        .transpose(0, 2, 1, 3)
        .reshape(shards, cand_slot * halves, DH)
    )
    exchange = functools.partial(
        lax.all_to_all, axis_name="req", split_axis=0, concat_axis=0, tiled=True
    )
    got_keys = exchange(pack(slots, cache_k, cand_rows))
    got_values = exchange(pack(slots, cache_v))

    own_out = lax.dynamic_slice_in_dim(
        lax.all_gather(w_out, "mp", axis=0, tiled=True), part * columns, columns, axis=1
    )

    home = hist_home[me]
    order = (jnp.arange(shards, dtype=jnp.int32) - home) % shards
    seen = jnp.take(hist_mask[0], order, axis=1, mode="clip").astype(jnp.float32)
    inside = order[:, None] * BLK + jnp.arange(BLK, dtype=jnp.int32)[None, :] < hist_len[0]
    mask = seen[:, :, None] * jnp.where(inside, 0.5 * DH**-0.5, 0.0)[None]
    mask = mask.reshape(hist_mask.shape[1], shards * BLK)

    arrived = (
        got_keys[:, 2 * BLK :, :]
        .reshape(shards, halves, cand_slot, DH)
        .transpose(0, 2, 1, 3)
        .reshape(cands, columns)
    )
    own_rows = jnp.take(arrived, cand_perm[0], axis=0, mode="clip")
    full_rows = lax.all_gather(own_rows, "mp", axis=1, tiled=True)
    gate, query, own = project(full_rows, w_in.reshape(w_in.shape[0], 4 * width), width)
    gates = lax.all_gather(gate, "mp", axis=0, tiled=False)

    weights = attention_weights(query, got_keys, mask)
    attn = weighted_values(weights, got_values, own, split)
    attn = lax.all_to_all(attn, "mp", split_axis=0, concat_axis=0, tiled=True)
    return finish(attn, gates, own_out, own_rows)


def solution(mesh):
    in_specs = (
        P("req", "mp"),
        P("req", None),
        P(None, None, "mp"),
        P("mp", None),
        P("req", None, "mp"),
        P("req", None, "mp"),
        P("req"),
        P(),
        P(),
        P("req", None, None),
    )
    out_specs = P("req", "mp")
    return jax.shard_map(local, mesh=mesh, in_specs=in_specs, out_specs=out_specs, check_vma=False)
```

```python
import functools

import jax
import jax.numpy as jnp
from jax import lax
from jax.experimental import pallas as pl
from jax.experimental.pallas import tpu as pltpu
from jax.sharding import PartitionSpec as P

HEADS = 8
DH = 128
BLK = 32
MAXBLK = 128
GROUP = 128
EPS = 1e-05
VMEM = 28 * 1024 * 1024
WHOLE = pl.BlockSpec(memory_space=pltpu.VMEM)
IN_HBM = pl.BlockSpec(memory_space=pltpu.HBM)


def hbm(x):
    return pltpu.with_memory_space_constraint(x, pltpu.HBM)


def cost(flops, nbytes, trans=0):
    return pl.CostEstimate(flops=flops, bytes_accessed=nbytes, transcendentals=trans)


def pack_kernel(slots, cache, *refs):
    out, held, made, load_sem, store_sem = refs[-5:]
    load = pltpu.make_async_copy(cache, held, load_sem)
    load.start()
    load.wait()
    shards, rows, _ = made.shape
    per = shards // store_sem.shape[0]
    stores = []
    for c in range(store_sem.shape[0]):
        chunk = pl.ds(c * per, per)
        for r in range(c * per, (c + 1) * per):
            block = held[slots[r]]
            made[r, :BLK, :] = block[:, :DH]
            made[r, BLK : 2 * BLK, :] = block[:, DH:]
        if rows > 2 * BLK:
            made[chunk, 2 * BLK :, :] = refs[0][chunk]
        stores.append(pltpu.make_async_copy(made.at[chunk], out.at[chunk], store_sem.at[c]))
        stores[-1].start()
    for store in stores:
        store.wait()


def pack(slots, cache, extra=None, after=()):
    shards = slots.shape[0]
    rows = 2 * BLK + (0 if extra is None else extra.shape[1])
    in_specs, args = [IN_HBM], [hbm(cache)]
    if extra is not None:
        in_specs.append(WHOLE)
        args.append(extra)
    in_specs += [pl.BlockSpec(memory_space=pl.ANY)] * len(after)
    out_shape = (shards, rows, DH)
    return pl.pallas_call(
        pack_kernel,
        out_shape=pltpu.HBM(out_shape, cache.dtype),
        in_specs=[pl.BlockSpec(memory_space=pltpu.SMEM)] + in_specs,
        out_specs=IN_HBM,
        scratch_shapes=[
            pltpu.VMEM(cache.shape, cache.dtype),
            pltpu.VMEM(out_shape, cache.dtype),
            pltpu.SemaphoreType.DMA,
            pltpu.SemaphoreType.DMA((4,)),
        ],
        compiler_params=pltpu.CompilerParams(vmem_limit_bytes=VMEM),
        cost_estimate=cost(0, 2 * shards * rows * DH * 2),
        name="pack",
    )(slots, *args, *after)


def silu(half):
    return half + half * jnp.tanh(half)


def project_kernel(part, r0, r1, r2, r3, w, g1, g2, g3, gates, query, own, normed):
    pieces = [r[...].astype(jnp.float32) for r in (r0, r1, r2, r3)]
    split = len(pieces)
    width = r0.shape[1]
    total = split * width
    mean = sum(jnp.sum(p, axis=1, keepdims=True) for p in pieces) / total
    centred = [p - mean for p in pieces]
    spread = sum(jnp.sum(c * c, axis=1, keepdims=True) for c in centred) / total
    scale = lax.rsqrt(spread + EPS)
    for d in range(split):
        at = pl.multiple_of(lax.rem(part[0] + (split - d), split) * width, width)
        normed[:, pl.ds(at, width)] = (centred[d] * scale).astype(jnp.bfloat16)
    x = normed[...]

    def times(matrix):
        return silu(0.5 * jnp.dot(x, matrix, preferred_element_type=jnp.float32)).astype(
            jnp.bfloat16
        )

    gates[0] = times(w[:, :width])
    for d, g in ((1, g1), (2, g2), (3, g3)):
        gates[d] = times(g[...])
    value = times(w[:, width : 2 * width]).astype(jnp.float32)
    q = times(w[:, 2 * width : 3 * width])
    query[...] = q
    key = times(w[:, 3 * width :]).astype(jnp.float32)
    product = q.astype(jnp.float32) * key
    for h in range(width // DH):
        cols = slice(h * DH, (h + 1) * DH)
        half = jnp.sum(product[:, cols], axis=1, keepdims=True) * (0.5 * DH**-0.5)
        own[:, cols] = silu(half) * value[:, cols]


def project(part, rows, w, gate_w):
    cands, width = rows[0].shape
    split = len(rows)
    depth = split * width
    step = 128
    block = pl.BlockSpec((step, width), lambda i, s: (i, 0))
    whole = lambda a: pl.BlockSpec(a.shape, lambda i, s: (0, 0))
    return pl.pallas_call(
        project_kernel,
        out_shape=(
            jax.ShapeDtypeStruct((split, cands, width), jnp.bfloat16),
            jax.ShapeDtypeStruct((cands, width), jnp.bfloat16),
            jax.ShapeDtypeStruct((cands, width), jnp.float32),
        ),
        grid_spec=pltpu.PrefetchScalarGridSpec(
            num_scalar_prefetch=1,
            grid=(cands // step,),
            in_specs=[block] * split + [whole(w)] + [whole(g) for g in gate_w],
            out_specs=(
                pl.BlockSpec((split, step, width), lambda i, s: (0, i, 0)),
                block,
                block,
            ),
            scratch_shapes=[pltpu.VMEM((step, depth), jnp.bfloat16)],
        ),
        compiler_params=pltpu.CompilerParams(vmem_limit_bytes=VMEM),
        cost_estimate=cost(2 * cands * depth * 7 * width, 8 << 20, cands * 7 * width),
        name="project",
    )(part, *rows, w, *gate_w)


def weights_kernel(query, keys, mask, out):
    sources = keys.shape[0]
    n = sources * BLK
    for h in range(query.shape[1] // DH):
        k = keys[:, h * BLK : (h + 1) * BLK, :].reshape(n, DH)
        for g in range(query.shape[0] // GROUP):
            rows = slice(g * GROUP, (g + 1) * GROUP)
            s = lax.dot_general(
                query[rows, h * DH : (h + 1) * DH],
                k,
                (((1,), (1,)), ((), ())),
                preferred_element_type=jnp.float32,
            )
            out[0, h, rows, :] = silu(s * mask[g : g + 1, :]).astype(jnp.bfloat16)


def attention_weights(query, got, mask):
    shards = got.shape[0]
    cands, width = query.shape
    heads = width // DH
    per = 16
    return pl.pallas_call(
        weights_kernel,
        out_shape=pltpu.HBM((shards // per, heads, cands, per * BLK), jnp.bfloat16),
        grid=(shards // per,),
        in_specs=[
            pl.BlockSpec((cands, width), lambda i: (0, 0)),
            pl.BlockSpec((per, 2 * BLK, DH), lambda i: (i, 0, 0)),
            pl.BlockSpec((mask.shape[0], per * BLK), lambda i: (0, i)),
        ],
        out_specs=pl.BlockSpec((1, heads, cands, per * BLK), lambda i: (i, 0, 0, 0)),
        compiler_params=pltpu.CompilerParams(vmem_limit_bytes=VMEM),
        cost_estimate=cost(
            2 * cands * shards * BLK * width, 12 << 20, heads * cands * shards * BLK
        ),
        name="weights",
    )(query, got, mask)


def values_kernel(weights, values, own, out, w, v, held, total, w_sem, v_sem, own_sem):
    steps, heads, cands, n = weights.shape
    per = n // BLK
    copies = out.shape[0]
    loads = []
    for c in range(steps):
        chunk = pl.ds(c * per, per)
        loads.append(
            [pltpu.make_async_copy(values.at[chunk], v.at[chunk], v_sem.at[c])]
            + [
                pltpu.make_async_copy(weights.at[c, h], w.at[c, h], w_sem.at[c, h])
                for h in range(heads)
            ]
        )
        for load in loads[-1]:
            load.start()
    last = pltpu.make_async_copy(own, held, own_sem)
    last.start()
    for c in range(steps):
        for load in loads[c]:
            load.wait()
        if c == steps - 1:
            last.wait()
        for h in range(heads):
            cols = slice(h * DH, (h + 1) * DH)
            part = jnp.dot(
                w[c, h],
                v[c * per : (c + 1) * per, h * BLK : (h + 1) * BLK, :].reshape(n, DH),
                preferred_element_type=jnp.float32,
            )
            if c == 0:
                total[:, cols] = part
            elif c < steps - 1:
                total[:, cols] += part
            else:
                done = (total[:, cols] + part + held[:, cols]).astype(jnp.bfloat16)
                for i in range(copies):
                    out[i, :, cols] = done


def weighted_values(weights, got, own, copies):
    shards = got.shape[0]
    steps, heads, cands, _ = weights.shape
    width = own.shape[1]
    return pl.pallas_call(
        values_kernel,
        out_shape=jax.ShapeDtypeStruct((copies, cands, width), jnp.bfloat16),
        in_specs=[IN_HBM, IN_HBM, IN_HBM],
        out_specs=WHOLE,
        scratch_shapes=[
            pltpu.VMEM(weights.shape, weights.dtype),
            pltpu.VMEM(got.shape, got.dtype),
            pltpu.VMEM(own.shape, own.dtype),
            pltpu.VMEM((cands, width), jnp.float32),
            pltpu.SemaphoreType.DMA((steps, heads)),
            pltpu.SemaphoreType.DMA((steps,)),
            pltpu.SemaphoreType.DMA,
        ],
        compiler_params=pltpu.CompilerParams(vmem_limit_bytes=VMEM),
        cost_estimate=cost(2 * cands * shards * BLK * width, 12 << 20),
        name="values",
    )(hbm(weights), hbm(got), hbm(own))


def finish_kernel(part, attn, gates, w0, w1, w2, w3, rows, out):
    split, _, width = attn.shape
    step = out.shape[0]
    here = pl.ds(pl.multiple_of(pl.program_id(0) * step, step), step)
    pieces = [
        attn[lax.rem(part[0] + (split - d), split), here, :].astype(jnp.float32)
        for d in range(split)
    ]
    total = split * width
    mean = jnp.sum(sum(pieces), axis=1, keepdims=True) / total
    centred = [p - mean for p in pieces]
    spread = jnp.sum(sum(c * c for c in centred), axis=1, keepdims=True) / total
    scale = lax.rsqrt(spread + EPS)
    result = rows[here, :].astype(jnp.float32)
    for d, w in enumerate((w0, w1, w2, w3)):
        hidden = (centred[d] * scale * gates[d, here, :].astype(jnp.float32)).astype(jnp.bfloat16)
        result += jnp.dot(hidden, w[...], preferred_element_type=jnp.float32)
    out[...] = result.astype(out.dtype)


def finish(part, attn, gates, ws, rows):
    split, cands, width = attn.shape
    step = 128
    return pl.pallas_call(
        finish_kernel,
        out_shape=jax.ShapeDtypeStruct(rows.shape, jnp.bfloat16),
        grid_spec=pltpu.PrefetchScalarGridSpec(
            num_scalar_prefetch=1,
            grid=(cands // step,),
            in_specs=[WHOLE] * (3 + len(ws)),
            out_specs=pl.BlockSpec((step, rows.shape[1]), lambda i, s: (i, 0)),
        ),
        compiler_params=pltpu.CompilerParams(vmem_limit_bytes=VMEM),
        cost_estimate=cost(2 * cands * split * width * rows.shape[1], 3 << 20),
        name="finish",
    )(part, attn, gates, *ws, rows)


def local(
    cand_feats, cand_perm, w_in, w_out, cache_k, cache_v, hist_len, hist_home, hist_slot, hist_mask
):
    shards = lax.axis_size("req")
    split = lax.axis_size("mp")
    me = lax.axis_index("req")
    part = lax.axis_index("mp")
    parts = part.astype(jnp.int32).reshape(1)
    columns = cand_feats.shape[1]
    cand_slot = cand_feats.shape[0] // shards
    cands = cand_perm.shape[1]
    width = w_in.shape[2]

    def back(x, d):
        return lax.ppermute(x, "mp", [(i, (i + d) % split) for i in range(split)])

    behind = me - hist_home
    wanted = jnp.where(behind < 0, behind + shards, behind)
    places = jnp.arange(MAXBLK, dtype=jnp.int32)
    slots = jnp.sum(jnp.where(places[None, :] == wanted[:, None], hist_slot, 0), axis=1)

    halves = columns // DH
    cand_rows = (
        cand_feats.reshape(shards, cand_slot, halves, DH)
        .transpose(0, 2, 1, 3)
        .reshape(shards, cand_slot * halves, DH)
    )
    exchange = functools.partial(
        lax.all_to_all, axis_name="req", split_axis=0, concat_axis=0, tiled=True
    )
    got_keys = exchange(pack(slots, cache_k, extra=cand_rows))

    w_gate = w_in[:, 0, :]
    gate_w = [back(w_gate, d) for d in range(1, split)]
    own_out = []
    for d in range(split):
        piece = lax.dynamic_slice_in_dim(w_out, (part + d) % split * columns, columns, axis=1)
        own_out.append(back(piece, d) if d else piece)

    home = hist_home[me]
    order = (jnp.arange(shards, dtype=jnp.int32) - home) % shards
    seen = jnp.take(hist_mask[0], order, axis=1, mode="clip").astype(jnp.float32)
    inside = order[:, None] * BLK + jnp.arange(BLK, dtype=jnp.int32)[None, :] < hist_len[0]
    mask = seen[:, :, None] * jnp.where(inside, 0.5 * DH**-0.5, 0.0)[None]
    mask = mask.reshape(hist_mask.shape[1], shards * BLK)

    w_flat = w_in.reshape(w_in.shape[0], 4 * width)
    ready = [*gate_w, *own_out, mask, w_flat]
    got_values = exchange(pack(slots, cache_v, after=ready))

    arrived = (
        got_keys[:, 2 * BLK :, :]
        .reshape(shards, halves, cand_slot, DH)
        .transpose(0, 2, 1, 3)
        .reshape(cands, columns)
    )
    own_rows = jnp.take(arrived, cand_perm[0], axis=0, mode="clip")
    rows = [own_rows] + [back(own_rows, d) for d in range(1, split)]
    gates, query, own = project(parts, rows, w_flat, gate_w)

    weights = attention_weights(query, got_keys, mask)
    attn = weighted_values(weights, got_values, own, split)
    attn = lax.all_to_all(attn, "mp", split_axis=0, concat_axis=0, tiled=True)
    return finish(parts, attn, gates, own_out, own_rows)


def solution(mesh):
    in_specs = (
        P("req", "mp"),
        P("req", None),
        P(None, None, "mp"),
        P("mp", None),
        P("req", None, "mp"),
        P("req", None, "mp"),
        P("req"),
        P(),
        P(),
        P("req", None, None),
    )
    out_specs = P("req", "mp")
    return jax.shard_map(local, mesh=mesh, in_specs=in_specs, out_specs=out_specs, check_vma=False)
```

```python
import functools

import jax
import jax.numpy as jnp
from jax import lax
from jax.experimental import pallas as pl
from jax.experimental.pallas import tpu as pltpu
from jax.sharding import PartitionSpec as P

HEADS = 8
DH = 128
BLK = 32
MAXBLK = 128
GROUP = 128
CSLOT = 4
EPS = 1e-05
VMEM = 28 * 1024 * 1024
WHOLE = pl.BlockSpec(memory_space=pltpu.VMEM)
IN_HBM = pl.BlockSpec(memory_space=pltpu.HBM)


def hbm(x):
    return pltpu.with_memory_space_constraint(x, pltpu.HBM)


def cost(flops, nbytes, trans=0):
    return pl.CostEstimate(flops=flops, bytes_accessed=nbytes, transcendentals=trans)


def spread_rows(rows_in):
    count, columns = rows_in.shape
    halves = columns // DH
    x = jnp.concatenate([rows_in[:, h * DH : (h + 1) * DH] for h in range(halves)], axis=0)
    shape = (halves * count, halves * count)
    at = lax.broadcasted_iota(jnp.int32, shape, 0)
    source = lax.broadcasted_iota(jnp.int32, shape, 1)
    group, inner = at // (CSLOT * halves), at % (CSLOT * halves)
    wanted = (inner // CSLOT) * count + group * CSLOT + inner % CSLOT
    pick = jnp.where(source == wanted, 1.0, 0.0).astype(jnp.bfloat16)
    return jnp.dot(pick, x, preferred_element_type=jnp.float32).astype(rows_in.dtype)


def pack_kernel(home_in, table_in, cache, *refs):
    out, home, table, held, made, cand, index_sem, load_sem, store_sem = refs[-9:]
    indices = [
        pltpu.make_async_copy(home_in, home, index_sem.at[0]),
        pltpu.make_async_copy(table_in, table, index_sem.at[1]),
    ]
    parts = load_sem.shape[0]
    size = cache.shape[0] // parts
    blocks = []
    for i in range(parts):
        at = pl.ds(i * size, size)
        blocks.append(pltpu.make_async_copy(cache.at[at], held.at[at], load_sem.at[i]))
    for load in indices:
        load.start()
    shards, rows, _ = made.shape
    if rows > 2 * BLK:
        extra = pltpu.make_async_copy(refs[0], cand, index_sem.at[2])
        extra.start()
    for load in blocks:
        load.start()
    if rows > 2 * BLK:
        extra.wait()
        step = 32
        for b in range(0, cand.shape[0], step):
            x = spread_rows(cand[b : b + step, :])
            n = step // CSLOT
            made[b // CSLOT : b // CSLOT + n, 2 * BLK :, :] = x.reshape(n, rows - 2 * BLK, DH)
    for load in indices + blocks:
        load.wait()
    me = lax.axis_index("req")
    per = shards // store_sem.shape[0]
    stores = []
    for c in range(store_sem.shape[0]):
        chunk = pl.ds(c * per, per)
        for r in range(c * per, (c + 1) * per):
            behind = me - home[r]
            block = held[table[r, jnp.where(behind < 0, behind + shards, behind)]]
            made[r, :BLK, :] = block[:, :DH]
            made[r, BLK : 2 * BLK, :] = block[:, DH:]
        stores.append(pltpu.make_async_copy(made.at[chunk], out.at[chunk], store_sem.at[c]))
        stores[-1].start()
    for store in stores:
        store.wait()


def pack(home, table, cache, cand=None, after=()):
    shards = home.shape[0]
    rows = 2 * BLK
    args = [hbm(home), hbm(table), hbm(cache)]
    held_cand = (16, DH)
    if cand is not None:
        rows += cand.shape[0] * cand.shape[1] // (DH * shards)
        args.append(hbm(cand))
        held_cand = cand.shape
    in_specs = [IN_HBM] * len(args) + [pl.BlockSpec(memory_space=pl.ANY)] * len(after)
    out_shape = (shards, rows, DH)
    return pl.pallas_call(
        pack_kernel,
        out_shape=pltpu.HBM(out_shape, cache.dtype),
        in_specs=in_specs,
        out_specs=IN_HBM,
        scratch_shapes=[
            pltpu.SMEM(home.shape, jnp.int32),
            pltpu.SMEM(table.shape, jnp.int32),
            pltpu.VMEM(cache.shape, cache.dtype),
            pltpu.VMEM(out_shape, cache.dtype),
            pltpu.VMEM(held_cand, cache.dtype),
            pltpu.SemaphoreType.DMA((3,)),
            pltpu.SemaphoreType.DMA((4,)),
            pltpu.SemaphoreType.DMA((4,)),
        ],
        compiler_params=pltpu.CompilerParams(vmem_limit_bytes=VMEM),
        cost_estimate=cost(0, 2 * shards * rows * DH * 2),
        name="pack",
    )(*args, *after)


def silu(half):
    return half + half * jnp.tanh(half)


def project_kernel(r0, r1, r2, r3, w, g1, g2, g3, gates, query, own, normed):
    pieces = [r[...].astype(jnp.float32) for r in (r0, r1, r2, r3)]
    split = len(pieces)
    width = r0.shape[1]
    total = split * width
    part = lax.axis_index("mp")
    place = [lax.rem(part + (split - d), split) for d in range(split)]
    mean = sum(jnp.sum(p, axis=1, keepdims=True) for p in pieces) / total
    centred = [p - mean for p in pieces]
    spread = sum(jnp.sum(c * c, axis=1, keepdims=True) for c in centred) / total
    scale = lax.rsqrt(spread + EPS)
    for d in range(split):
        at = pl.multiple_of(place[d] * width, width)
        normed[:, pl.ds(at, width)] = (centred[d] * scale).astype(jnp.bfloat16)
    x = normed[...]

    def times(matrix):
        return silu(0.5 * jnp.dot(x, matrix, preferred_element_type=jnp.float32)).astype(
            jnp.bfloat16
        )

    gates[place[0]] = times(w[:, :width])
    for d, g in ((1, g1), (2, g2), (3, g3)):
        gates[place[d]] = times(g[...])
    value = times(w[:, width : 2 * width]).astype(jnp.float32)
    q = times(w[:, 2 * width : 3 * width])
    query[...] = q
    key = times(w[:, 3 * width :]).astype(jnp.float32)
    product = q.astype(jnp.float32) * key
    for h in range(width // DH):
        cols = slice(h * DH, (h + 1) * DH)
        half = jnp.sum(product[:, cols], axis=1, keepdims=True) * (0.5 * DH**-0.5)
        own[:, cols] = silu(half) * value[:, cols]


def project(rows, w, gate_w):
    cands, width = rows[0].shape
    split = len(rows)
    depth = split * width
    step = 128
    block = pl.BlockSpec((step, width), lambda i: (i, 0))
    whole = lambda a: pl.BlockSpec(a.shape, lambda i: (0, 0))
    return pl.pallas_call(
        project_kernel,
        out_shape=(
            jax.ShapeDtypeStruct((split, cands, width), jnp.bfloat16),
            jax.ShapeDtypeStruct((cands, width), jnp.bfloat16),
            pltpu.HBM((cands, width), jnp.float32),
        ),
        grid=(cands // step,),
        in_specs=[block] * split + [whole(w)] + [whole(g) for g in gate_w],
        out_specs=(
            pl.BlockSpec((split, step, width), lambda i: (0, i, 0)),
            block,
            block,
        ),
        scratch_shapes=[pltpu.VMEM((step, depth), jnp.bfloat16)],
        compiler_params=pltpu.CompilerParams(vmem_limit_bytes=VMEM),
        cost_estimate=cost(2 * cands * depth * 7 * width, 8 << 20, cands * 7 * width),
        name="project",
    )(*[hbm(r) for r in rows], hbm(w), *[hbm(g) for g in gate_w])


def weights_kernel(query, keys, mask, out):
    sources = keys.shape[0]
    n = sources * BLK
    for h in range(query.shape[1] // DH):
        k = keys[:, h * BLK : (h + 1) * BLK, :].reshape(n, DH)
        for g in range(query.shape[0] // GROUP):
            rows = slice(g * GROUP, (g + 1) * GROUP)
            s = lax.dot_general(
                query[rows, h * DH : (h + 1) * DH],
                k,
                (((1,), (1,)), ((), ())),
                preferred_element_type=jnp.float32,
            )
            out[0, h, rows, :] = silu(s * mask[g : g + 1, :]).astype(jnp.bfloat16)


def attention_weights(query, got, mask):
    shards = got.shape[0]
    cands, width = query.shape
    heads = width // DH
    per = 16
    return pl.pallas_call(
        weights_kernel,
        out_shape=pltpu.HBM((shards // per, heads, cands, per * BLK), jnp.bfloat16),
        grid=(shards // per,),
        in_specs=[
            pl.BlockSpec((cands, width), lambda i: (0, 0)),
            pl.BlockSpec((per, 2 * BLK, DH), lambda i: (i, 0, 0)),
            pl.BlockSpec((mask.shape[0], per * BLK), lambda i: (0, i)),
        ],
        out_specs=pl.BlockSpec((1, heads, cands, per * BLK), lambda i: (i, 0, 0, 0)),
        compiler_params=pltpu.CompilerParams(vmem_limit_bytes=VMEM),
        cost_estimate=cost(
            2 * cands * shards * BLK * width, 12 << 20, heads * cands * shards * BLK
        ),
        name="weights",
    )(query, got, mask)


def values_kernel(weights, values, own, out, w, v, held, total, w_sem, v_sem, own_sem):
    steps, heads, cands, n = weights.shape
    per = n // BLK
    copies = out.shape[0]
    loads = []
    for c in range(steps):
        chunk = pl.ds(c * per, per)
        loads.append(
            [pltpu.make_async_copy(values.at[chunk], v.at[chunk], v_sem.at[c])]
            + [
                pltpu.make_async_copy(weights.at[c, h], w.at[c, h], w_sem.at[c, h])
                for h in range(heads)
            ]
        )
        for load in loads[-1]:
            load.start()
    last = pltpu.make_async_copy(own, held, own_sem)
    last.start()
    for c in range(steps):
        for load in loads[c]:
            load.wait()
        if c == steps - 1:
            last.wait()
        for h in range(heads):
            cols = slice(h * DH, (h + 1) * DH)
            part = jnp.dot(
                w[c, h],
                v[c * per : (c + 1) * per, h * BLK : (h + 1) * BLK, :].reshape(n, DH),
                preferred_element_type=jnp.float32,
            )
            if c == 0:
                total[:, cols] = part
            elif c < steps - 1:
                total[:, cols] += part
            else:
                done = (total[:, cols] + part + held[:, cols]).astype(jnp.bfloat16)
                for i in range(copies):
                    out[i, :, cols] = done


def weighted_values(weights, got, own, copies):
    shards = got.shape[0]
    steps, heads, cands, _ = weights.shape
    width = own.shape[1]
    return pl.pallas_call(
        values_kernel,
        out_shape=jax.ShapeDtypeStruct((copies, cands, width), jnp.bfloat16),
        in_specs=[IN_HBM, IN_HBM, IN_HBM],
        out_specs=WHOLE,
        scratch_shapes=[
            pltpu.VMEM(weights.shape, weights.dtype),
            pltpu.VMEM(got.shape, got.dtype),
            pltpu.VMEM(own.shape, own.dtype),
            pltpu.VMEM((cands, width), jnp.float32),
            pltpu.SemaphoreType.DMA((steps, heads)),
            pltpu.SemaphoreType.DMA((steps,)),
            pltpu.SemaphoreType.DMA,
        ],
        compiler_params=pltpu.CompilerParams(vmem_limit_bytes=VMEM),
        cost_estimate=cost(2 * cands * shards * BLK * width, 12 << 20),
        name="values",
    )(hbm(weights), hbm(got), hbm(own))


def finish_kernel(attn, gates, w, rows, out, made, sems):
    split, cands, width = attn.shape
    total = split * width
    count = sems.shape[0]
    step = cands // count
    stores = []
    for b in range(count):
        here = slice(b * step, (b + 1) * step)
        pieces = [attn[i, here, :].astype(jnp.float32) for i in range(split)]
        mean = jnp.sum(sum(pieces), axis=1, keepdims=True) / total
        centred = [p - mean for p in pieces]
        spread = jnp.sum(sum(c * c for c in centred), axis=1, keepdims=True) / total
        scale = lax.rsqrt(spread + EPS)
        hidden = jnp.concatenate(
            [
                (centred[i] * scale * gates[i, here, :].astype(jnp.float32)).astype(jnp.bfloat16)
                for i in range(split)
            ],
            axis=1,
        )
        result = rows[here, :].astype(jnp.float32) + jnp.dot(
            hidden, w[...], preferred_element_type=jnp.float32
        )
        made[here, :] = result.astype(made.dtype)
        at = pl.ds(b * step, step)
        stores.append(pltpu.make_async_copy(made.at[at], out.at[at], sems.at[b]))
        stores[-1].start()
    for store in stores:
        store.wait()


def finish(attn, gates, w, rows):
    split, cands, width = attn.shape
    return pl.pallas_call(
        finish_kernel,
        out_shape=pltpu.HBM(rows.shape, jnp.bfloat16),
        in_specs=[WHOLE] * 4,
        out_specs=IN_HBM,
        scratch_shapes=[
            pltpu.VMEM(rows.shape, jnp.bfloat16),
            pltpu.SemaphoreType.DMA((4,)),
        ],
        compiler_params=pltpu.CompilerParams(vmem_limit_bytes=VMEM),
        cost_estimate=cost(2 * cands * split * width * rows.shape[1], 3 << 20),
        name="finish",
    )(attn, gates, w, rows)


def local(
    cand_feats, cand_perm, w_in, w_out, cache_k, cache_v, hist_len, hist_home, hist_slot, hist_mask
):
    shards = lax.axis_size("req")
    split = lax.axis_size("mp")
    me = lax.axis_index("req")
    part = lax.axis_index("mp")
    columns = cand_feats.shape[1]
    halves = columns // DH
    cand_slot = cand_feats.shape[0] // shards
    cands = cand_perm.shape[1]
    width = w_in.shape[2]

    def back(x, d):
        return lax.ppermute(x, "mp", [(i, (i + d) % split) for i in range(split)])

    exchange = functools.partial(
        lax.all_to_all, axis_name="req", split_axis=0, concat_axis=0, tiled=True
    )
    got_keys = exchange(pack(hist_home, hist_slot, cache_k, cand=cand_feats))

    w_gate = w_in[:, 0, :]
    gate_w = [back(w_gate, d) for d in range(1, split)]
    own_out = []
    for d in range(split):
        piece = lax.dynamic_slice_in_dim(w_out, (part + d) % split * columns, columns, axis=1)
        own_out.append(back(piece, d) if d else piece)
    backs = (part - jnp.arange(split, dtype=jnp.int32)) % split
    own_out = jnp.take(jnp.stack(own_out), backs, axis=0, mode="clip")
    own_out = own_out.reshape(split * columns, columns)

    home = hist_home[me]
    order = (jnp.arange(shards, dtype=jnp.int32) - home) % shards
    seen = jnp.take(hist_mask[0], order, axis=1, mode="clip").astype(jnp.float32)
    inside = order[:, None] * BLK + jnp.arange(BLK, dtype=jnp.int32)[None, :] < hist_len[0]
    mask = seen[:, :, None] * jnp.where(inside, 0.5 * DH**-0.5, 0.0)[None]
    mask = mask.reshape(hist_mask.shape[1], shards * BLK)

    w_flat = w_in.reshape(w_in.shape[0], 4 * width)
    ready = [*gate_w, own_out, mask, w_flat]
    got_values = exchange(pack(hist_home, hist_slot, cache_v, after=ready))

    arrived = (
        got_keys[:, 2 * BLK :, :]
        .reshape(shards, halves, cand_slot, DH)
        .transpose(0, 2, 1, 3)
        .reshape(cands, columns)
    )
    own_rows = jnp.take(arrived, cand_perm[0], axis=0, mode="clip")
    rows = [own_rows] + [back(own_rows, d) for d in range(1, split)]
    gates, query, own = project(rows, w_flat, gate_w)

    weights = attention_weights(query, got_keys, mask)
    attn = weighted_values(weights, got_values, own, split)
    attn = lax.all_to_all(attn, "mp", split_axis=0, concat_axis=0, tiled=True)
    return finish(attn, gates, own_out, own_rows)


def solution(mesh):
    in_specs = (
        P("req", "mp"),
        P("req", None),
        P(None, None, "mp"),
        P("mp", None),
        P("req", None, "mp"),
        P("req", None, "mp"),
        P("req"),
        P(),
        P(),
        P("req", None, None),
    )
    out_specs = P("req", "mp")
    return jax.shard_map(local, mesh=mesh, in_specs=in_specs, out_specs=out_specs, check_vma=False)
```

```python
import functools

import jax
import jax.numpy as jnp
from jax import lax
from jax.experimental import pallas as pl
from jax.experimental.pallas import tpu as pltpu
from jax.sharding import PartitionSpec as P

HEADS = 8
DH = 128
BLK = 32
MAXBLK = 128
GROUP = 128
CSLOT = 4
PER = 32
EPS = 1e-05
VMEM = 28 * 1024 * 1024
WHOLE = pl.BlockSpec(memory_space=pltpu.VMEM)
IN_HBM = pl.BlockSpec(memory_space=pltpu.HBM)


def hbm(x):
    return pltpu.with_memory_space_constraint(x, pltpu.HBM)


def cost(flops, nbytes, trans=0):
    return pl.CostEstimate(flops=flops, bytes_accessed=nbytes, transcendentals=trans)


def spread_rows(rows_in):
    count, columns = rows_in.shape
    halves = columns // DH
    x = jnp.concatenate([rows_in[:, h * DH : (h + 1) * DH] for h in range(halves)], axis=0)
    shape = (halves * count, halves * count)
    at = lax.broadcasted_iota(jnp.int32, shape, 0)
    source = lax.broadcasted_iota(jnp.int32, shape, 1)
    group, inner = at // (CSLOT * halves), at % (CSLOT * halves)
    wanted = (inner // CSLOT) * count + group * CSLOT + inner % CSLOT
    pick = jnp.where(source == wanted, 1.0, 0.0).astype(jnp.bfloat16)
    return jnp.dot(pick, x, preferred_element_type=jnp.float32).astype(rows_in.dtype)


def copy_kernel_inputs(pairs, sems):
    copies = [pltpu.make_async_copy(a, b, sems.at[i]) for i, (a, b) in enumerate(pairs)]
    for copy in copies:
        copy.start()
    return copies


def send_rows(home, table, made, out, store_sem, fill):
    shards = made.shape[0]
    me = lax.axis_index("req")
    per = shards // store_sem.shape[0]
    stores = []
    for c in range(store_sem.shape[0]):
        chunk = pl.ds(c * per, per)
        for r in range(c * per, (c + 1) * per):
            behind = me - home[r]
            fill(r, table[r, jnp.where(behind < 0, behind + shards, behind)])
        stores.append(pltpu.make_async_copy(made.at[chunk], out.at[chunk], store_sem.at[c]))
        stores[-1].start()
    for store in stores:
        store.wait()


def first_pack_kernel(
    home_in, table_in, keys_in, values_in, cand_in, out, home, table, keys, values, cand, made, sem, store_sem
):
    head = BLK // 2
    size = keys.shape[0] // 4
    loads = copy_kernel_inputs(
        [
            (cand_in, cand),
            (home_in, home),
            (table_in, table),
            (values_in.at[:, pl.ds(0, head), pl.ds(0, DH)], values),
        ]
        + [(keys_in.at[pl.ds(i * size, size)], keys.at[pl.ds(i * size, size)]) for i in range(4)],
        sem,
    )
    loads[0].wait()
    rows = made.shape[1]
    first = 2 * BLK + head
    step = 32
    for b in range(0, cand.shape[0], step):
        x = spread_rows(cand[b : b + step, :])
        n = step // CSLOT
        made[b // CSLOT : b // CSLOT + n, first:, :] = x.reshape(n, rows - first, DH)
    for load in loads[1:]:
        load.wait()

    def fill(r, slot):
        block = keys[slot]
        made[r, :BLK, :] = block[:, :DH]
        made[r, BLK : 2 * BLK, :] = block[:, DH:]
        made[r, 2 * BLK : first, :] = values[slot]

    send_rows(home, table, made, out, store_sem, fill)


def first_pack(home, table, keys, values, cand):
    shards = home.shape[0]
    rows = 2 * BLK + BLK // 2 + cand.shape[0] * cand.shape[1] // (DH * shards)
    out_shape = (shards, rows, DH)
    return pl.pallas_call(
        first_pack_kernel,
        out_shape=pltpu.HBM(out_shape, keys.dtype),
        in_specs=[IN_HBM] * 5,
        out_specs=IN_HBM,
        scratch_shapes=[
            pltpu.SMEM(home.shape, jnp.int32),
            pltpu.SMEM(table.shape, jnp.int32),
            pltpu.VMEM(keys.shape, keys.dtype),
            pltpu.VMEM((values.shape[0], BLK // 2, DH), keys.dtype),
            pltpu.VMEM(cand.shape, cand.dtype),
            pltpu.VMEM(out_shape, keys.dtype),
            pltpu.SemaphoreType.DMA((8,)),
            pltpu.SemaphoreType.DMA((4,)),
        ],
        compiler_params=pltpu.CompilerParams(vmem_limit_bytes=VMEM),
        cost_estimate=cost(0, 2 * shards * rows * DH * 2),
        name="first_pack",
    )(hbm(home), hbm(table), hbm(keys), hbm(values), hbm(cand))


def second_pack_kernel(home_in, table_in, values_in, *refs):
    out, home, table, values, made, sem, store_sem = refs[-7:]
    for load in copy_kernel_inputs(
        [(home_in, home), (table_in, table), (values_in, values)], sem
    ):
        load.wait()
    head = BLK // 2

    def fill(r, slot):
        block = values[slot]
        made[r, :head, :] = block[head:, :DH]
        made[r, head:, :] = block[:, DH:]

    send_rows(home, table, made, out, store_sem, fill)


def second_pack(home, table, values, after):
    shards = home.shape[0]
    out_shape = (shards, BLK + BLK // 2, DH)
    return pl.pallas_call(
        second_pack_kernel,
        out_shape=pltpu.HBM(out_shape, values.dtype),
        in_specs=[IN_HBM] * 3 + [pl.BlockSpec(memory_space=pl.ANY)] * len(after),
        out_specs=IN_HBM,
        scratch_shapes=[
            pltpu.SMEM(home.shape, jnp.int32),
            pltpu.SMEM(table.shape, jnp.int32),
            pltpu.VMEM(values.shape, values.dtype),
            pltpu.VMEM(out_shape, values.dtype),
            pltpu.SemaphoreType.DMA((3,)),
            pltpu.SemaphoreType.DMA((4,)),
        ],
        compiler_params=pltpu.CompilerParams(vmem_limit_bytes=VMEM),
        cost_estimate=cost(0, 2 * shards * out_shape[1] * DH * 2),
        name="second_pack",
    )(hbm(home), hbm(table), hbm(values), *after)


def silu(half):
    return half + half * jnp.tanh(half)


def project_kernel(r0, r1, r2, r3, w, g1, g2, g3, gates, query, own, normed):
    pieces = [r[...].astype(jnp.float32) for r in (r0, r1, r2, r3)]
    split = len(pieces)
    width = r0.shape[1]
    total = split * width
    part = lax.axis_index("mp")
    place = [lax.rem(part + (split - d), split) for d in range(split)]
    mean = sum(jnp.sum(p, axis=1, keepdims=True) for p in pieces) / total
    centred = [p - mean for p in pieces]
    spread = sum(jnp.sum(c * c, axis=1, keepdims=True) for c in centred) / total
    scale = lax.rsqrt(spread + EPS)
    for d in range(split):
        at = pl.multiple_of(place[d] * width, width)
        normed[:, pl.ds(at, width)] = (centred[d] * scale).astype(jnp.bfloat16)
    x = normed[...]

    def times(matrix):
        return silu(0.5 * jnp.dot(x, matrix, preferred_element_type=jnp.float32)).astype(
            jnp.bfloat16
        )

    gates[place[0]] = times(w[:, :width])
    for d, g in ((1, g1), (2, g2), (3, g3)):
        gates[place[d]] = times(g[...])
    value = times(w[:, width : 2 * width]).astype(jnp.float32)
    q = times(w[:, 2 * width : 3 * width])
    query[...] = q
    key = times(w[:, 3 * width :]).astype(jnp.float32)
    product = q.astype(jnp.float32) * key
    for h in range(width // DH):
        cols = slice(h * DH, (h + 1) * DH)
        half = jnp.sum(product[:, cols], axis=1, keepdims=True) * (0.5 * DH**-0.5)
        own[:, cols] = silu(half) * value[:, cols]


def project(rows, w, gate_w):
    cands, width = rows[0].shape
    split = len(rows)
    depth = split * width
    step = 128
    block = pl.BlockSpec((step, width), lambda i: (i, 0))
    whole = lambda a: pl.BlockSpec(a.shape, lambda i: (0, 0))
    return pl.pallas_call(
        project_kernel,
        out_shape=(
            jax.ShapeDtypeStruct((split, cands, width), jnp.bfloat16),
            jax.ShapeDtypeStruct((cands, width), jnp.bfloat16),
            pltpu.HBM((cands, width), jnp.float32),
        ),
        grid=(cands // step,),
        in_specs=[block] * split + [whole(w)] + [whole(g) for g in gate_w],
        out_specs=(
            pl.BlockSpec((split, step, width), lambda i: (0, i, 0)),
            block,
            block,
        ),
        scratch_shapes=[pltpu.VMEM((step, depth), jnp.bfloat16)],
        compiler_params=pltpu.CompilerParams(vmem_limit_bytes=VMEM),
        cost_estimate=cost(2 * cands * depth * 7 * width, 8 << 20, cands * 7 * width),
        name="project",
    )(*[hbm(r) for r in rows], hbm(w), *[hbm(g) for g in gate_w])


def head_weights(query, keys, mask):
    s = lax.dot_general(query, keys, (((1,), (1,)), ((), ())), preferred_element_type=jnp.float32)
    return silu(s * mask).astype(jnp.bfloat16)


def half_rows(blocks, i):
    half = BLK // 2
    part = blocks[:, i * half : (i + 1) * half, :]
    return part.reshape(part.shape[0] * half, DH)


def weights_kernel(query, got, mask, own, out, base, early):
    n = PER * BLK // 2

    @pl.when(pl.program_id(0) == 0)
    def _():
        base[...] = own[...]

    for h in range(query.shape[1] // DH):
        a, b = half_rows(got, 2 * h), half_rows(got, 2 * h + 1)
        for g in range(query.shape[0] // GROUP):
            rows = slice(g * GROUP, (g + 1) * GROUP)
            q = query[rows, h * DH : (h + 1) * DH]
            at = mask[g : g + 1, :]
            w_a, w_b = head_weights(q, a, at[:, :n]), head_weights(q, b, at[:, n:])
            if h == 0:
                early[rows, :] = w_a
                out[0, rows, :n] = w_b
            else:
                out[0, rows, n : 2 * n] = w_a
                out[0, rows, 2 * n :] = w_b
    base[:, :DH] += jnp.dot(early[...], half_rows(got, 4), preferred_element_type=jnp.float32)


def attention_weights(query, got, mask, own):
    steps = got.shape[0] // PER
    cands, width = query.shape
    n = PER * BLK
    whole = lambda a: pl.BlockSpec(a.shape, lambda i: (0, 0))
    return pl.pallas_call(
        weights_kernel,
        out_shape=(
            pltpu.HBM((steps, cands, 3 * n // 2), jnp.bfloat16),
            pltpu.HBM((cands, width), jnp.float32),
        ),
        grid=(steps,),
        in_specs=[
            whole(query),
            pl.BlockSpec((PER, 2 * BLK + BLK // 2, DH), lambda i: (i, 0, 0)),
            pl.BlockSpec((mask.shape[0], n), lambda i: (0, i)),
            whole(own),
        ],
        out_specs=(pl.BlockSpec((1, cands, 3 * n // 2), lambda i: (i, 0, 0)), whole(own)),
        scratch_shapes=[pltpu.VMEM((cands, n // 2), jnp.bfloat16)],
        compiler_params=pltpu.CompilerParams(vmem_limit_bytes=VMEM),
        cost_estimate=cost(
            2 * cands * steps * n * width, 12 << 20, steps * cands * n * width // DH
        ),
        name="weights",
    )(query, got, mask, own)


def values_kernel(weights, values, base, out, w, v, held, total, w_sem, v_sem, base_sem):
    steps, cands, count = weights.shape
    n = count // 3
    loads = []
    for c in range(steps):
        chunk = pl.ds(c * PER, PER)
        loads.append(
            (
                pltpu.make_async_copy(values.at[chunk], v.at[chunk], v_sem.at[c]),
                pltpu.make_async_copy(weights.at[pl.ds(c, 1)], w.at[pl.ds(c, 1)], w_sem.at[c]),
            )
        )
        for load in loads[-1]:
            load.start()
    last = pltpu.make_async_copy(base, held, base_sem)
    last.start()
    for c in range(steps):
        for load in loads[c]:
            load.wait()
        if c == steps - 1:
            last.wait()
        blocks = v[c * PER : (c + 1) * PER]
        for h, pieces in enumerate(((0,), (1, 2))):
            cols = slice(h * DH, (h + 1) * DH)
            part = sum(
                jnp.dot(
                    w[c, :, i * n : (i + 1) * n],
                    half_rows(blocks, i),
                    preferred_element_type=jnp.float32,
                )
                for i in pieces
            )
            if c == 0:
                total[:, cols] = part
            elif c < steps - 1:
                total[:, cols] += part
            else:
                done = (total[:, cols] + part + held[:, cols]).astype(jnp.bfloat16)
                for i in range(out.shape[0]):
                    out[i, :, cols] = done


def weighted_values(weights, got, base, copies):
    steps = weights.shape[0]
    cands, width = base.shape
    return pl.pallas_call(
        values_kernel,
        out_shape=jax.ShapeDtypeStruct((copies, cands, width), jnp.bfloat16),
        in_specs=[IN_HBM] * 3,
        out_specs=WHOLE,
        scratch_shapes=[
            pltpu.VMEM(weights.shape, weights.dtype),
            pltpu.VMEM(got.shape, got.dtype),
            pltpu.VMEM(base.shape, base.dtype),
            pltpu.VMEM((cands, width), jnp.float32),
            pltpu.SemaphoreType.DMA((steps,)),
            pltpu.SemaphoreType.DMA((steps,)),
            pltpu.SemaphoreType.DMA,
        ],
        compiler_params=pltpu.CompilerParams(vmem_limit_bytes=VMEM),
        cost_estimate=cost(2 * weights.size * DH, 12 << 20),
        name="values",
    )(hbm(weights), hbm(got), hbm(base))


def finish_kernel(attn, gates, w, rows, out, made, sems):
    split, cands, width = attn.shape
    total = split * width
    count = sems.shape[0]
    step = cands // count
    stores = []
    for b in range(count):
        here = slice(b * step, (b + 1) * step)
        pieces = [attn[i, here, :].astype(jnp.float32) for i in range(split)]
        mean = jnp.sum(sum(pieces), axis=1, keepdims=True) / total
        centred = [p - mean for p in pieces]
        spread = jnp.sum(sum(c * c for c in centred), axis=1, keepdims=True) / total
        scale = lax.rsqrt(spread + EPS)
        hidden = jnp.concatenate(
            [
                (centred[i] * scale * gates[i, here, :].astype(jnp.float32)).astype(jnp.bfloat16)
                for i in range(split)
            ],
            axis=1,
        )
        result = rows[here, :].astype(jnp.float32) + jnp.dot(
            hidden, w[...], preferred_element_type=jnp.float32
        )
        made[here, :] = result.astype(made.dtype)
        at = pl.ds(b * step, step)
        stores.append(pltpu.make_async_copy(made.at[at], out.at[at], sems.at[b]))
        stores[-1].start()
    for store in stores:
        store.wait()


def finish(attn, gates, w, rows):
    split, cands, width = attn.shape
    return pl.pallas_call(
        finish_kernel,
        out_shape=pltpu.HBM(rows.shape, jnp.bfloat16),
        in_specs=[WHOLE] * 4,
        out_specs=IN_HBM,
        scratch_shapes=[
            pltpu.VMEM(rows.shape, jnp.bfloat16),
            pltpu.SemaphoreType.DMA((4,)),
        ],
        compiler_params=pltpu.CompilerParams(vmem_limit_bytes=VMEM),
        cost_estimate=cost(2 * cands * split * width * rows.shape[1], 3 << 20),
        name="finish",
    )(attn, gates, w, rows)


def local(
    cand_feats, cand_perm, w_in, w_out, cache_k, cache_v, hist_len, hist_home, hist_slot, hist_mask
):
    shards = lax.axis_size("req")
    split = lax.axis_size("mp")
    me = lax.axis_index("req")
    part = lax.axis_index("mp")
    columns = cand_feats.shape[1]
    halves = columns // DH
    cand_slot = cand_feats.shape[0] // shards
    cands = cand_perm.shape[1]
    width = w_in.shape[2]

    def back(x, d):
        return lax.ppermute(x, "mp", [(i, (i + d) % split) for i in range(split)])

    exchange = functools.partial(
        lax.all_to_all, axis_name="req", split_axis=0, concat_axis=0, tiled=True
    )
    got_first = exchange(first_pack(hist_home, hist_slot, cache_k, cache_v, cand_feats))

    w_gate = w_in[:, 0, :]
    gate_w = [back(w_gate, d) for d in range(1, split)]
    own_out = []
    for d in range(split):
        piece = lax.dynamic_slice_in_dim(w_out, (part + d) % split * columns, columns, axis=1)
        own_out.append(back(piece, d) if d else piece)
    backs = (part - jnp.arange(split, dtype=jnp.int32)) % split
    own_out = jnp.take(jnp.stack(own_out), backs, axis=0, mode="clip")
    own_out = own_out.reshape(split * columns, columns)

    chunks, half = shards // PER, BLK // 2
    home = hist_home[me]
    order = (jnp.arange(shards, dtype=jnp.int32) - home) % shards
    seen = jnp.take(hist_mask[0], order, axis=1, mode="clip").astype(jnp.float32)
    place = jnp.arange(BLK, dtype=jnp.int32).reshape(2, 1, half)
    inside = order.reshape(chunks, 1, PER, 1) * BLK + place < hist_len[0]
    mask = seen.reshape(-1, chunks, 1, PER, 1) * jnp.where(inside, 0.5 * DH**-0.5, 0.0)[None]
    mask = mask.reshape(hist_mask.shape[1], shards * BLK)

    w_flat = w_in.reshape(w_in.shape[0], 4 * width)
    ready = [*gate_w, own_out, mask, w_flat]
    got_second = exchange(second_pack(hist_home, hist_slot, cache_v, ready))

    arrived = (
        got_first[:, 2 * BLK + half :, :]
        .reshape(shards, halves, cand_slot, DH)
        .transpose(0, 2, 1, 3)
        .reshape(cands, columns)
    )
    own_rows = jnp.take(arrived, cand_perm[0], axis=0, mode="clip")
    rows = [own_rows] + [back(own_rows, d) for d in range(1, split)]
    gates, query, own = project(rows, w_flat, gate_w)

    weights, base = attention_weights(query, got_first, mask, own)
    attn = weighted_values(weights, got_second, base, split)
    attn = lax.all_to_all(attn, "mp", split_axis=0, concat_axis=0, tiled=True)
    return finish(attn, gates, own_out, own_rows)


def solution(mesh):
    in_specs = (
        P("req", "mp"),
        P("req", None),
        P(None, None, "mp"),
        P("mp", None),
        P("req", None, "mp"),
        P("req", None, "mp"),
        P("req"),
        P(),
        P(),
        P("req", None, None),
    )
    out_specs = P("req", "mp")
    return jax.shard_map(local, mesh=mesh, in_specs=in_specs, out_specs=out_specs, check_vma=False)
```

```python
import functools

import jax
import jax.numpy as jnp
from jax import lax
from jax.experimental import pallas as pl
from jax.experimental.pallas import tpu as pltpu
from jax.sharding import PartitionSpec as P

HEADS = 8
DH = 128
BLK = 32
MAXBLK = 128
GROUP = 128
CSLOT = 4
PER = 32
EPS = 1e-05
VMEM = 28 * 1024 * 1024
WHOLE = pl.BlockSpec(memory_space=pltpu.VMEM)
IN_HBM = pl.BlockSpec(memory_space=pltpu.HBM)


def hbm(x):
    return pltpu.with_memory_space_constraint(x, pltpu.HBM)


def cost(flops, nbytes, trans=0):
    return pl.CostEstimate(flops=flops, bytes_accessed=nbytes, transcendentals=trans)


def spread_rows(rows_in):
    count, columns = rows_in.shape
    halves = columns // DH
    x = jnp.concatenate([rows_in[:, h * DH : (h + 1) * DH] for h in range(halves)], axis=0)
    shape = (halves * count, halves * count)
    at = lax.broadcasted_iota(jnp.int32, shape, 0)
    source = lax.broadcasted_iota(jnp.int32, shape, 1)
    group, inner = at // (CSLOT * halves), at % (CSLOT * halves)
    wanted = (inner // CSLOT) * count + group * CSLOT + inner % CSLOT
    pick = jnp.where(source == wanted, 1.0, 0.0).astype(jnp.bfloat16)
    return jnp.dot(pick, x, preferred_element_type=jnp.float32).astype(rows_in.dtype)


def pack_kernel(head, with_rows, home_in, table_in, keys_in, values_in, *refs):
    out, home, table, keys, values, cand, made, index_sem, load_sem, store_sem = refs[-10:]
    cols = pl.ds(head * DH, DH)
    pairs = [(home_in, home), (table_in, table)]
    if with_rows:
        pairs.append((refs[0], cand))
    indices = [pltpu.make_async_copy(a, b, index_sem.at[i]) for i, (a, b) in enumerate(pairs)]
    blocks = [
        pltpu.make_async_copy(a.at[:, :, cols], b, load_sem.at[i])
        for i, (a, b) in enumerate(((keys_in, keys), (values_in, values)))
    ]
    for load in indices[2:] + indices[:2] + blocks:
        load.start()
    shards, rows, _ = made.shape
    if with_rows:
        indices[2].wait()
        step = 32
        for b in range(0, cand.shape[0], step):
            x = spread_rows(cand[b : b + step, :])
            n = step // CSLOT
            made[b // CSLOT : b // CSLOT + n, 2 * BLK :, :] = x.reshape(n, rows - 2 * BLK, DH)
    for load in indices[:2] + blocks:
        load.wait()
    me = lax.axis_index("req")
    per = shards // store_sem.shape[0]
    stores = []
    for c in range(store_sem.shape[0]):
        chunk = pl.ds(c * per, per)
        for r in range(c * per, (c + 1) * per):
            behind = me - home[r]
            slot = table[r, jnp.where(behind < 0, behind + shards, behind)]
            made[r, :BLK, :] = keys[slot]
            made[r, BLK : 2 * BLK, :] = values[slot]
        stores.append(pltpu.make_async_copy(made.at[chunk], out.at[chunk], store_sem.at[c]))
        stores[-1].start()
    for store in stores:
        store.wait()


def pack(head, home, table, keys, values, cand=None, after=()):
    shards = home.shape[0]
    rows = 2 * BLK
    args = [hbm(home), hbm(table), hbm(keys), hbm(values)]
    held_cand = (16, DH)
    if cand is not None:
        rows += cand.shape[0] * cand.shape[1] // (DH * shards)
        args.append(hbm(cand))
        held_cand = cand.shape
    out_shape = (shards, rows, DH)
    held = (keys.shape[0], BLK, DH)
    return pl.pallas_call(
        functools.partial(pack_kernel, head, cand is not None),
        out_shape=pltpu.HBM(out_shape, keys.dtype),
        in_specs=[IN_HBM] * len(args) + [pl.BlockSpec(memory_space=pl.ANY)] * len(after),
        out_specs=IN_HBM,
        scratch_shapes=[
            pltpu.SMEM(home.shape, jnp.int32),
            pltpu.SMEM(table.shape, jnp.int32),
            pltpu.VMEM(held, keys.dtype),
            pltpu.VMEM(held, keys.dtype),
            pltpu.VMEM(held_cand, keys.dtype),
            pltpu.VMEM(out_shape, keys.dtype),
            pltpu.SemaphoreType.DMA((3,)),
            pltpu.SemaphoreType.DMA((2,)),
            pltpu.SemaphoreType.DMA((4,)),
        ],
        compiler_params=pltpu.CompilerParams(vmem_limit_bytes=VMEM),
        cost_estimate=cost(0, 2 * shards * rows * DH * 2),
        name="pack",
    )(*args, *after)


def silu(half):
    return half + half * jnp.tanh(half)


def project_kernel(r0, r1, r2, r3, w, g1, g2, g3, gates, query, own, normed):
    pieces = [r[...].astype(jnp.float32) for r in (r0, r1, r2, r3)]
    split = len(pieces)
    width = r0.shape[1]
    total = split * width
    part = lax.axis_index("mp")
    place = [lax.rem(part + (split - d), split) for d in range(split)]
    mean = sum(jnp.sum(p, axis=1, keepdims=True) for p in pieces) / total
    centred = [p - mean for p in pieces]
    spread = sum(jnp.sum(c * c, axis=1, keepdims=True) for c in centred) / total
    scale = lax.rsqrt(spread + EPS)
    for d in range(split):
        at = pl.multiple_of(place[d] * width, width)
        normed[:, pl.ds(at, width)] = (centred[d] * scale).astype(jnp.bfloat16)
    x = normed[...]

    def times(matrix):
        return silu(0.5 * jnp.dot(x, matrix, preferred_element_type=jnp.float32)).astype(
            jnp.bfloat16
        )

    gates[place[0]] = times(w[:, :width])
    for d, g in ((1, g1), (2, g2), (3, g3)):
        gates[place[d]] = times(g[...])
    value = times(w[:, width : 2 * width]).astype(jnp.float32)
    q = times(w[:, 2 * width : 3 * width])
    key = times(w[:, 3 * width :]).astype(jnp.float32)
    product = q.astype(jnp.float32) * key
    for h in range(width // DH):
        cols = slice(h * DH, (h + 1) * DH)
        half = jnp.sum(product[:, cols], axis=1, keepdims=True) * (0.5 * DH**-0.5)
        own[h] = silu(half) * value[:, cols]
        query[h] = q[:, cols]


def project(rows, w, gate_w):
    cands, width = rows[0].shape
    split = len(rows)
    depth = split * width
    step = 256
    heads = width // DH
    block = pl.BlockSpec((step, width), lambda i: (i, 0))
    by_head = pl.BlockSpec((heads, step, DH), lambda i: (0, i, 0))
    whole = lambda a: pl.BlockSpec(a.shape, lambda i: (0, 0))
    return pl.pallas_call(
        project_kernel,
        out_shape=(
            jax.ShapeDtypeStruct((split, cands, width), jnp.bfloat16),
            pltpu.HBM((heads, cands, DH), jnp.bfloat16),
            pltpu.HBM((heads, cands, DH), jnp.float32),
        ),
        grid=(cands // step,),
        in_specs=[block] * split + [whole(w)] + [whole(g) for g in gate_w],
        out_specs=(
            pl.BlockSpec((split, step, width), lambda i: (0, i, 0)),
            by_head,
            by_head,
        ),
        scratch_shapes=[pltpu.VMEM((step, depth), jnp.bfloat16)],
        compiler_params=pltpu.CompilerParams(vmem_limit_bytes=VMEM),
        cost_estimate=cost(2 * cands * depth * 7 * width, 8 << 20, cands * 7 * width),
        name="project",
    )(*[hbm(r) for r in rows], hbm(w), *[hbm(g) for g in gate_w])


def attend_kernel(query, got, mask, own, *refs):
    out, weights, total = refs[-3:]
    step = pl.program_id(0)
    n = got.shape[0] * BLK
    keys = got[:, :BLK, :].reshape(n, DH)
    for g in range(weights.shape[0] // GROUP):
        rows = slice(g * GROUP, (g + 1) * GROUP)
        s = lax.dot_general(
            query[0, rows, :], keys, (((1,), (1,)), ((), ())), preferred_element_type=jnp.float32
        )
        weights[rows, :] = silu(s * mask[g : g + 1, :]).astype(jnp.bfloat16)
    part = jnp.dot(
        weights[...], got[:, BLK : 2 * BLK, :].reshape(n, DH), preferred_element_type=jnp.float32
    )

    @pl.when(step == 0)
    def _():
        total[...] = own[0] + part

    @pl.when(step > 0)
    def _():
        total[...] += part

    @pl.when(step == pl.num_programs(0) - 1)
    def _():
        done = total[...].astype(jnp.bfloat16)
        for i in range(out.shape[0]):
            out[i] = done


def attend(head, query, got, mask, own, copies, after=()):
    shards = got.shape[0]
    _, cands, _ = query.shape
    n = PER * BLK
    of_head = pl.BlockSpec((1, cands, DH), lambda i: (head, 0, 0))
    return pl.pallas_call(
        attend_kernel,
        out_shape=jax.ShapeDtypeStruct((copies, cands, DH), jnp.bfloat16),
        grid=(shards // PER,),
        in_specs=[
            of_head,
            pl.BlockSpec((PER, 2 * BLK, DH), lambda i: (i, 0, 0)),
            pl.BlockSpec((mask.shape[0], n), lambda i: (0, i)),
            of_head,
        ]
        + [pl.BlockSpec(memory_space=pl.ANY)] * len(after),
        out_specs=pl.BlockSpec((copies, cands, DH), lambda i: (0, 0, 0)),
        scratch_shapes=[
            pltpu.VMEM((cands, n), jnp.bfloat16),
            pltpu.VMEM((cands, DH), jnp.float32),
        ],
        compiler_params=pltpu.CompilerParams(vmem_limit_bytes=VMEM),
        cost_estimate=cost(4 * cands * shards * BLK * DH, 4 << 20, cands * shards * BLK),
        name="attend",
    )(hbm(query), hbm(got), hbm(mask), hbm(own), *after)


def finish_kernel(a0, a1, a2, a3, last, gates, w, rows, out, made, sems):
    split, cands, width = gates.shape
    total = split * width
    count = sems.shape[0]
    step = cands // count
    part = lax.axis_index("mp")
    place = [lax.rem(part + (split - d), split) for d in range(split)]
    stores = []
    for b in range(count):
        here = slice(b * step, (b + 1) * step)
        pieces = [
            jnp.concatenate([a[0, here, :], last[place[d], here, :]], axis=1).astype(jnp.float32)
            for d, a in enumerate((a0, a1, a2, a3))
        ]
        mean = jnp.sum(sum(pieces), axis=1, keepdims=True) / total
        centred = [p - mean for p in pieces]
        spread = jnp.sum(sum(c * c for c in centred), axis=1, keepdims=True) / total
        scale = lax.rsqrt(spread + EPS)
        result = rows[here, :].astype(jnp.float32)
        for d in range(split):
            gate = gates[place[d], here, :].astype(jnp.float32)
            result += jnp.dot(
                (centred[d] * scale * gate).astype(jnp.bfloat16),
                w[place[d]],
                preferred_element_type=jnp.float32,
            )
        made[here, :] = result.astype(made.dtype)
        at = pl.ds(b * step, step)
        stores.append(pltpu.make_async_copy(made.at[at], out.at[at], sems.at[b]))
        stores[-1].start()
    for store in stores:
        store.wait()


def finish(firsts, last, gates, w, rows):
    split, cands, width = gates.shape
    return pl.pallas_call(
        finish_kernel,
        out_shape=pltpu.HBM(rows.shape, jnp.bfloat16),
        in_specs=[WHOLE] * (len(firsts) + 4),
        out_specs=IN_HBM,
        scratch_shapes=[
            pltpu.VMEM(rows.shape, jnp.bfloat16),
            pltpu.SemaphoreType.DMA((4,)),
        ],
        compiler_params=pltpu.CompilerParams(vmem_limit_bytes=VMEM),
        cost_estimate=cost(2 * cands * split * width * rows.shape[1], 3 << 20),
        name="finish",
    )(*firsts, last, gates, w, rows)


def local(
    cand_feats, cand_perm, w_in, w_out, cache_k, cache_v, hist_len, hist_home, hist_slot, hist_mask
):
    shards = lax.axis_size("req")
    split = lax.axis_size("mp")
    me = lax.axis_index("req")
    part = lax.axis_index("mp")
    columns = cand_feats.shape[1]
    halves = columns // DH
    cand_slot = cand_feats.shape[0] // shards
    cands = cand_perm.shape[1]
    width = w_in.shape[2]

    def back(x, d):
        return lax.ppermute(x, "mp", [(i, (i + d) % split) for i in range(split)])

    exchange = functools.partial(
        lax.all_to_all, axis_name="req", split_axis=0, concat_axis=0, tiled=True
    )
    history = (hist_home, hist_slot, cache_k, cache_v)
    got_first = exchange(pack(0, *history, cand=cand_feats))

    w_gate = w_in[:, 0, :]
    gate_w = [back(w_gate, d) for d in range(1, split)]
    own_out = []
    for d in range(split):
        piece = lax.dynamic_slice_in_dim(w_out, (part + d) % split * columns, columns, axis=1)
        own_out.append(back(piece, d) if d else piece)
    backs = (part - jnp.arange(split, dtype=jnp.int32)) % split
    own_out = jnp.take(jnp.stack(own_out), backs, axis=0, mode="clip")

    home = hist_home[me]
    order = (jnp.arange(shards, dtype=jnp.int32) - home) % shards
    seen = jnp.take(hist_mask[0], order, axis=1, mode="clip").astype(jnp.float32)
    inside = order[:, None] * BLK + jnp.arange(BLK, dtype=jnp.int32)[None, :] < hist_len[0]
    mask = seen[:, :, None] * jnp.where(inside, 0.5 * DH**-0.5, 0.0)[None]
    mask = mask.reshape(hist_mask.shape[1], shards * BLK)

    w_flat = w_in.reshape(w_in.shape[0], 4 * width)
    ready = [*gate_w, own_out, mask, w_flat]
    got_second = exchange(pack(1, *history, after=ready))

    arrived = (
        got_first[:, 2 * BLK :, :]
        .reshape(shards, halves, cand_slot, DH)
        .transpose(0, 2, 1, 3)
        .reshape(cands, columns)
    )
    own_rows = jnp.take(arrived, cand_perm[0], axis=0, mode="clip")
    rows = [own_rows] + [back(own_rows, d) for d in range(1, split)]
    gates, query, own = project(rows, w_flat, gate_w)

    first = attend(0, query, got_first, mask, own, 1)
    firsts = [first] + [back(first, d) for d in range(1, split)]
    last = attend(1, query, got_second, mask, own, split, after=firsts[1:])
    last = lax.all_to_all(last, "mp", split_axis=0, concat_axis=0, tiled=True)
    return finish(firsts, last, gates, own_out, own_rows)


def solution(mesh):
    in_specs = (
        P("req", "mp"),
        P("req", None),
        P(None, None, "mp"),
        P("mp", None),
        P("req", None, "mp"),
        P("req", None, "mp"),
        P("req"),
        P(),
        P(),
        P("req", None, None),
    )
    out_specs = P("req", "mp")
    return jax.shard_map(local, mesh=mesh, in_specs=in_specs, out_specs=out_specs, check_vma=False)
```

```python
import functools

import jax
import jax.numpy as jnp
from jax import lax
from jax.experimental import pallas as pl
from jax.experimental.pallas import tpu as pltpu
from jax.sharding import PartitionSpec as P

HEADS = 8
DH = 128
BLK = 32
MAXBLK = 128
GROUP = 128
CSLOT = 4
PER = 64
EPS = 1e-05
VMEM = 28 * 1024 * 1024
WHOLE = pl.BlockSpec(memory_space=pltpu.VMEM)
IN_HBM = pl.BlockSpec(memory_space=pltpu.HBM)


def hbm(x):
    return pltpu.with_memory_space_constraint(x, pltpu.HBM)


def cost(flops, nbytes, trans=0):
    return pl.CostEstimate(flops=flops, bytes_accessed=nbytes, transcendentals=trans)


def spread_rows(rows_in):
    count, columns = rows_in.shape
    halves = columns // DH
    x = jnp.concatenate([rows_in[:, h * DH : (h + 1) * DH] for h in range(halves)], axis=0)
    shape = (halves * count, halves * count)
    at = lax.broadcasted_iota(jnp.int32, shape, 0)
    source = lax.broadcasted_iota(jnp.int32, shape, 1)
    group, inner = at // (CSLOT * halves), at % (CSLOT * halves)
    wanted = (inner // CSLOT) * count + group * CSLOT + inner % CSLOT
    pick = jnp.where(source == wanted, 1.0, 0.0).astype(jnp.bfloat16)
    return jnp.dot(pick, x, preferred_element_type=jnp.float32).astype(rows_in.dtype)


def pack_kernel(head, with_rows, home_in, table_in, keys_in, values_in, *refs):
    out, home, table, keys, values, cand, made, index_sem, load_sem, store_sem = refs[-10:]
    cols = pl.ds(head * DH, DH)
    pairs = [(home_in, home), (table_in, table)]
    if with_rows:
        pairs.append((refs[0], cand))
    indices = [pltpu.make_async_copy(a, b, index_sem.at[i]) for i, (a, b) in enumerate(pairs)]
    blocks = [
        pltpu.make_async_copy(a.at[:, :, cols], b, load_sem.at[i])
        for i, (a, b) in enumerate(((keys_in, keys), (values_in, values)))
    ]
    for load in indices[2:] + indices[:2] + blocks:
        load.start()
    shards, rows, _ = made.shape
    if with_rows:
        indices[2].wait()
        step = 32
        for b in range(0, cand.shape[0], step):
            x = spread_rows(cand[b : b + step, :])
            n = step // CSLOT
            made[b // CSLOT : b // CSLOT + n, 2 * BLK :, :] = x.reshape(n, rows - 2 * BLK, DH)
    for load in indices[:2] + blocks:
        load.wait()
    me = lax.axis_index("req")
    per = shards // store_sem.shape[0]
    stores = []
    for c in range(store_sem.shape[0]):
        chunk = pl.ds(c * per, per)
        for r in range(c * per, (c + 1) * per):
            behind = me - home[r]
            slot = table[r, jnp.where(behind < 0, behind + shards, behind)]
            made[r, :BLK, :] = keys[slot]
            made[r, BLK : 2 * BLK, :] = values[slot]
        stores.append(pltpu.make_async_copy(made.at[chunk], out.at[chunk], store_sem.at[c]))
        stores[-1].start()
    for store in stores:
        store.wait()


def pack(head, home, table, keys, values, cand=None, after=()):
    shards = home.shape[0]
    rows = 2 * BLK
    args = [hbm(home), hbm(table), hbm(keys), hbm(values)]
    held_cand = (16, DH)
    if cand is not None:
        rows += cand.shape[0] * cand.shape[1] // (DH * shards)
        args.append(hbm(cand))
        held_cand = cand.shape
    out_shape = (shards, rows, DH)
    held = (keys.shape[0], BLK, DH)
    return pl.pallas_call(
        functools.partial(pack_kernel, head, cand is not None),
        out_shape=pltpu.HBM(out_shape, keys.dtype),
        in_specs=[IN_HBM] * len(args) + [pl.BlockSpec(memory_space=pl.ANY)] * len(after),
        out_specs=IN_HBM,
        scratch_shapes=[
            pltpu.SMEM(home.shape, jnp.int32),
            pltpu.SMEM(table.shape, jnp.int32),
            pltpu.VMEM(held, keys.dtype),
            pltpu.VMEM(held, keys.dtype),
            pltpu.VMEM(held_cand, keys.dtype),
            pltpu.VMEM(out_shape, keys.dtype),
            pltpu.SemaphoreType.DMA((3,)),
            pltpu.SemaphoreType.DMA((2,)),
            pltpu.SemaphoreType.DMA((4,)),
        ],
        compiler_params=pltpu.CompilerParams(vmem_limit_bytes=VMEM),
        cost_estimate=cost(0, 2 * shards * rows * DH * 2),
        name="pack",
    )(*args, *after)


def silu(half):
    return half + half * jnp.tanh(half)


def project_kernel(r0, r1, r2, r3, w, g1, g2, g3, gates, query, own, normed):
    pieces = [r[...].astype(jnp.float32) for r in (r0, r1, r2, r3)]
    split = len(pieces)
    width = r0.shape[1]
    total = split * width
    part = lax.axis_index("mp")
    place = [lax.rem(part + (split - d), split) for d in range(split)]
    mean = sum(jnp.sum(p, axis=1, keepdims=True) for p in pieces) / total
    centred = [p - mean for p in pieces]
    spread = sum(jnp.sum(c * c, axis=1, keepdims=True) for c in centred) / total
    scale = lax.rsqrt(spread + EPS)
    for d in range(split):
        at = pl.multiple_of(place[d] * width, width)
        normed[:, pl.ds(at, width)] = (centred[d] * scale).astype(jnp.bfloat16)
    x = normed[...]

    def times(matrix):
        return silu(0.5 * jnp.dot(x, matrix, preferred_element_type=jnp.float32)).astype(
            jnp.bfloat16
        )

    gates[place[0]] = times(w[:, :width])
    for d, g in ((1, g1), (2, g2), (3, g3)):
        gates[place[d]] = times(g[...])
    value = times(w[:, width : 2 * width]).astype(jnp.float32)
    q = times(w[:, 2 * width : 3 * width])
    key = times(w[:, 3 * width :]).astype(jnp.float32)
    product = q.astype(jnp.float32) * key
    for h in range(width // DH):
        cols = slice(h * DH, (h + 1) * DH)
        half = jnp.sum(product[:, cols], axis=1, keepdims=True) * (0.5 * DH**-0.5)
        own[h] = silu(half) * value[:, cols]
        query[h] = q[:, cols]


def project(rows, w, gate_w):
    cands, width = rows[0].shape
    split = len(rows)
    depth = split * width
    step = 256
    heads = width // DH
    block = pl.BlockSpec((step, width), lambda i: (i, 0))
    by_head = pl.BlockSpec((heads, step, DH), lambda i: (0, i, 0))
    whole = lambda a: pl.BlockSpec(a.shape, lambda i: (0, 0))
    return pl.pallas_call(
        project_kernel,
        out_shape=(
            jax.ShapeDtypeStruct((split, cands, width), jnp.bfloat16),
            pltpu.HBM((heads, cands, DH), jnp.bfloat16),
            pltpu.HBM((heads, cands, DH), jnp.float32),
        ),
        grid=(cands // step,),
        in_specs=[block] * split + [whole(w)] + [whole(g) for g in gate_w],
        out_specs=(
            pl.BlockSpec((split, step, width), lambda i: (0, i, 0)),
            by_head,
            by_head,
        ),
        scratch_shapes=[pltpu.VMEM((step, depth), jnp.bfloat16)],
        compiler_params=pltpu.CompilerParams(vmem_limit_bytes=VMEM),
        cost_estimate=cost(2 * cands * depth * 7 * width, 8 << 20, cands * 7 * width),
        name="project",
    )(*[hbm(r) for r in rows], hbm(w), *[hbm(g) for g in gate_w])


def attend_kernel(query, got, mask, own, *refs):
    out, weights, total = refs[-3:]
    step = pl.program_id(0)
    n = got.shape[0] * BLK
    keys = got[:, :BLK, :].reshape(n, DH)
    for g in range(weights.shape[0] // GROUP):
        rows = slice(g * GROUP, (g + 1) * GROUP)
        s = lax.dot_general(
            query[0, rows, :], keys, (((1,), (1,)), ((), ())), preferred_element_type=jnp.float32
        )
        weights[rows, :] = silu(s * mask[g : g + 1, :]).astype(jnp.bfloat16)
    part = jnp.dot(
        weights[...], got[:, BLK : 2 * BLK, :].reshape(n, DH), preferred_element_type=jnp.float32
    )

    @pl.when(step == 0)
    def _():
        total[...] = own[0] + part

    @pl.when(step > 0)
    def _():
        total[...] += part

    @pl.when(step == pl.num_programs(0) - 1)
    def _():
        done = total[...].astype(jnp.bfloat16)
        for i in range(out.shape[0]):
            out[i] = done


def attend(head, query, got, mask, own, copies, after=()):
    shards = got.shape[0]
    _, cands, _ = query.shape
    n = PER * BLK
    of_head = pl.BlockSpec((1, cands, DH), lambda i: (head, 0, 0))
    return pl.pallas_call(
        attend_kernel,
        out_shape=jax.ShapeDtypeStruct((copies, cands, DH), jnp.bfloat16),
        grid=(shards // PER,),
        in_specs=[
            of_head,
            pl.BlockSpec((PER, 2 * BLK, DH), lambda i: (i, 0, 0)),
            pl.BlockSpec((mask.shape[0], n), lambda i: (0, i)),
            of_head,
        ]
        + [pl.BlockSpec(memory_space=pl.ANY)] * len(after),
        out_specs=pl.BlockSpec((copies, cands, DH), lambda i: (0, 0, 0)),
        scratch_shapes=[
            pltpu.VMEM((cands, n), jnp.bfloat16),
            pltpu.VMEM((cands, DH), jnp.float32),
        ],
        compiler_params=pltpu.CompilerParams(vmem_limit_bytes=VMEM),
        cost_estimate=cost(4 * cands * shards * BLK * DH, 4 << 20, cands * shards * BLK),
        name="attend",
    )(hbm(query), hbm(got), hbm(mask), hbm(own), *after)


def finish_kernel(a0, a1, a2, a3, last, gates, w, rows, out, made, sems):
    split, cands, width = gates.shape
    total = split * width
    count = sems.shape[0]
    step = cands // count
    part = lax.axis_index("mp")
    place = [lax.rem(part + (split - d), split) for d in range(split)]
    stores = []
    for b in range(count):
        here = slice(b * step, (b + 1) * step)
        pieces = [
            jnp.concatenate([a[0, here, :], last[place[d], here, :]], axis=1).astype(jnp.float32)
            for d, a in enumerate((a0, a1, a2, a3))
        ]
        mean = jnp.sum(sum(pieces), axis=1, keepdims=True) / total
        centred = [p - mean for p in pieces]
        spread = jnp.sum(sum(c * c for c in centred), axis=1, keepdims=True) / total
        scale = lax.rsqrt(spread + EPS)
        result = rows[here, :].astype(jnp.float32)
        for d in range(split):
            gate = gates[place[d], here, :].astype(jnp.float32)
            result += jnp.dot(
                (centred[d] * scale * gate).astype(jnp.bfloat16),
                w[place[d]],
                preferred_element_type=jnp.float32,
            )
        made[here, :] = result.astype(made.dtype)
        at = pl.ds(b * step, step)
        stores.append(pltpu.make_async_copy(made.at[at], out.at[at], sems.at[b]))
        stores[-1].start()
    for store in stores:
        store.wait()


def finish(firsts, last, gates, w, rows):
    split, cands, width = gates.shape
    return pl.pallas_call(
        finish_kernel,
        out_shape=pltpu.HBM(rows.shape, jnp.bfloat16),
        in_specs=[WHOLE] * (len(firsts) + 4),
        out_specs=IN_HBM,
        scratch_shapes=[
            pltpu.VMEM(rows.shape, jnp.bfloat16),
            pltpu.SemaphoreType.DMA((4,)),
        ],
        compiler_params=pltpu.CompilerParams(vmem_limit_bytes=VMEM),
        cost_estimate=cost(2 * cands * split * width * rows.shape[1], 3 << 20),
        name="finish",
    )(*firsts, last, gates, w, rows)


def local(
    cand_feats, cand_perm, w_in, w_out, cache_k, cache_v, hist_len, hist_home, hist_slot, hist_mask
):
    shards = lax.axis_size("req")
    split = lax.axis_size("mp")
    me = lax.axis_index("req")
    part = lax.axis_index("mp")
    columns = cand_feats.shape[1]
    halves = columns // DH
    cand_slot = cand_feats.shape[0] // shards
    cands = cand_perm.shape[1]
    width = w_in.shape[2]

    def back(x, d):
        return lax.ppermute(x, "mp", [(i, (i + d) % split) for i in range(split)])

    exchange = functools.partial(
        lax.all_to_all, axis_name="req", split_axis=0, concat_axis=0, tiled=True
    )
    history = (hist_home, hist_slot, cache_k, cache_v)
    got_first = exchange(pack(0, *history, cand=cand_feats))

    w_gate = w_in[:, 0, :]
    gate_w = [back(w_gate, d) for d in range(1, split)]
    own_out = []
    for d in range(split):
        piece = lax.dynamic_slice_in_dim(w_out, (part + d) % split * columns, columns, axis=1)
        own_out.append(back(piece, d) if d else piece)
    backs = (part - jnp.arange(split, dtype=jnp.int32)) % split
    own_out = jnp.take(jnp.stack(own_out), backs, axis=0, mode="clip")

    home = hist_home[me]
    order = (jnp.arange(shards, dtype=jnp.int32) - home) % shards
    seen = jnp.take(hist_mask[0], order, axis=1, mode="clip").astype(jnp.float32)
    inside = order[:, None] * BLK + jnp.arange(BLK, dtype=jnp.int32)[None, :] < hist_len[0]
    mask = seen[:, :, None] * jnp.where(inside, 0.5 * DH**-0.5, 0.0)[None]
    mask = mask.reshape(hist_mask.shape[1], shards * BLK)

    w_flat = w_in.reshape(w_in.shape[0], 4 * width)
    ready = [*gate_w, own_out, mask, w_flat]
    got_second = exchange(pack(1, *history, after=ready))

    arrived = (
        got_first[:, 2 * BLK :, :]
        .reshape(shards, halves, cand_slot, DH)
        .transpose(0, 2, 1, 3)
        .reshape(cands, columns)
    )
    own_rows = jnp.take(arrived, cand_perm[0], axis=0, mode="clip")
    rows = [own_rows] + [back(own_rows, d) for d in range(1, split)]
    gates, query, own = project(rows, w_flat, gate_w)

    first = attend(0, query, got_first, mask, own, 1)
    firsts = [first] + [back(first, d) for d in range(1, split)]
    last = attend(1, query, got_second, mask, own, split, after=firsts[1:])
    last = lax.all_to_all(last, "mp", split_axis=0, concat_axis=0, tiled=True)
    return finish(firsts, last, gates, own_out, own_rows)


def solution(mesh):
    in_specs = (
        P("req", "mp"),
        P("req", None),
        P(None, None, "mp"),
        P("mp", None),
        P("req", None, "mp"),
        P("req", None, "mp"),
        P("req"),
        P(),
        P(),
        P("req", None, None),
    )
    out_specs = P("req", "mp")
    return jax.shard_map(local, mesh=mesh, in_specs=in_specs, out_specs=out_specs, check_vma=False)
```

```python
import functools

import jax
import jax.numpy as jnp
from jax import lax
from jax.experimental import pallas as pl
from jax.experimental.pallas import tpu as pltpu
from jax.sharding import PartitionSpec as P

HEADS = 8
DH = 128
BLK = 32
MAXBLK = 128
GROUP = 128
CSLOT = 4
PER = 64
EPS = 1e-05
VMEM = 28 * 1024 * 1024
WHOLE = pl.BlockSpec(memory_space=pltpu.VMEM)
IN_HBM = pl.BlockSpec(memory_space=pltpu.HBM)


def hbm(x):
    return pltpu.with_memory_space_constraint(x, pltpu.HBM)


def cost(flops, nbytes, trans=0):
    return pl.CostEstimate(flops=flops, bytes_accessed=nbytes, transcendentals=trans)


def spread_rows(rows_in):
    count, columns = rows_in.shape
    halves = columns // DH
    x = jnp.concatenate([rows_in[:, h * DH : (h + 1) * DH] for h in range(halves)], axis=0)
    shape = (halves * count, halves * count)
    at = lax.broadcasted_iota(jnp.int32, shape, 0)
    source = lax.broadcasted_iota(jnp.int32, shape, 1)
    group, inner = at // (CSLOT * halves), at % (CSLOT * halves)
    wanted = (inner // CSLOT) * count + group * CSLOT + inner % CSLOT
    pick = jnp.where(source == wanted, 1.0, 0.0).astype(jnp.bfloat16)
    return jnp.dot(pick, x, preferred_element_type=jnp.float32).astype(rows_in.dtype)


def pack_kernel(head, with_rows, home_in, table_in, keys_in, values_in, *refs):
    out, home, table, keys, values, cand, made, index_sem, load_sem, store_sem = refs[-10:]
    cols = pl.ds(head * DH, DH)
    pairs = [(home_in, home), (table_in, table)]
    if with_rows:
        pairs.append((refs[0], cand))
    indices = [pltpu.make_async_copy(a, b, index_sem.at[i]) for i, (a, b) in enumerate(pairs)]
    blocks = [
        pltpu.make_async_copy(a.at[:, :, cols], b, load_sem.at[i])
        for i, (a, b) in enumerate(((keys_in, keys), (values_in, values)))
    ]
    for load in indices[2:] + indices[:2] + blocks:
        load.start()
    shards, rows, _ = made.shape
    if with_rows:
        indices[2].wait()
        step = 32
        for b in range(0, cand.shape[0], step):
            x = spread_rows(cand[b : b + step, :])
            n = step // CSLOT
            made[b // CSLOT : b // CSLOT + n, 2 * BLK :, :] = x.reshape(n, rows - 2 * BLK, DH)
    for load in indices[:2] + blocks:
        load.wait()
    me = lax.axis_index("req")
    per = shards // store_sem.shape[0]
    stores = []
    for c in range(store_sem.shape[0]):
        chunk = pl.ds(c * per, per)
        for r in range(c * per, (c + 1) * per):
            behind = me - home[r]
            slot = table[r, jnp.where(behind < 0, behind + shards, behind)]
            made[r, :BLK, :] = keys[slot]
            made[r, BLK : 2 * BLK, :] = values[slot]
        stores.append(pltpu.make_async_copy(made.at[chunk], out.at[chunk], store_sem.at[c]))
        stores[-1].start()
    for store in stores:
        store.wait()


def pack(head, home, table, keys, values, cand=None, after=()):
    shards = home.shape[0]
    rows = 2 * BLK
    args = [hbm(home), hbm(table), hbm(keys), hbm(values)]
    held_cand = (16, DH)
    if cand is not None:
        rows += cand.shape[0] * cand.shape[1] // (DH * shards)
        args.append(hbm(cand))
        held_cand = cand.shape
    out_shape = (shards, rows, DH)
    held = (keys.shape[0], BLK, DH)
    return pl.pallas_call(
        functools.partial(pack_kernel, head, cand is not None),
        out_shape=pltpu.HBM(out_shape, keys.dtype),
        in_specs=[IN_HBM] * len(args) + [pl.BlockSpec(memory_space=pl.ANY)] * len(after),
        out_specs=IN_HBM,
        scratch_shapes=[
            pltpu.SMEM(home.shape, jnp.int32),
            pltpu.SMEM(table.shape, jnp.int32),
            pltpu.VMEM(held, keys.dtype),
            pltpu.VMEM(held, keys.dtype),
            pltpu.VMEM(held_cand, keys.dtype),
            pltpu.VMEM(out_shape, keys.dtype),
            pltpu.SemaphoreType.DMA((3,)),
            pltpu.SemaphoreType.DMA((2,)),
            pltpu.SemaphoreType.DMA((8,)),
        ],
        compiler_params=pltpu.CompilerParams(vmem_limit_bytes=VMEM),
        cost_estimate=cost(0, 2 * shards * rows * DH * 2),
        name="pack",
    )(*args, *after)


def silu(half):
    return half + half * jnp.tanh(half)


def project_kernel(r0, r1, r2, r3, w, g1, g2, g3, gates, query, own, normed):
    pieces = [r[...].astype(jnp.float32) for r in (r0, r1, r2, r3)]
    split = len(pieces)
    width = r0.shape[1]
    total = split * width
    part = lax.axis_index("mp")
    place = [lax.rem(part + (split - d), split) for d in range(split)]
    mean = sum(jnp.sum(p, axis=1, keepdims=True) for p in pieces) / total
    centred = [p - mean for p in pieces]
    spread = sum(jnp.sum(c * c, axis=1, keepdims=True) for c in centred) / total
    scale = lax.rsqrt(spread + EPS)
    for d in range(split):
        at = pl.multiple_of(place[d] * width, width)
        normed[:, pl.ds(at, width)] = (centred[d] * scale).astype(jnp.bfloat16)
    x = normed[...]

    def times(matrix):
        return silu(0.5 * jnp.dot(x, matrix, preferred_element_type=jnp.float32)).astype(
            jnp.bfloat16
        )

    gates[place[0]] = times(w[:, :width])
    for d, g in ((1, g1), (2, g2), (3, g3)):
        gates[place[d]] = times(g[...])
    value = times(w[:, width : 2 * width]).astype(jnp.float32)
    q = times(w[:, 2 * width : 3 * width])
    key = times(w[:, 3 * width :]).astype(jnp.float32)
    product = q.astype(jnp.float32) * key
    for h in range(width // DH):
        cols = slice(h * DH, (h + 1) * DH)
        half = jnp.sum(product[:, cols], axis=1, keepdims=True) * (0.5 * DH**-0.5)
        own[h] = silu(half) * value[:, cols]
        query[h] = q[:, cols]


def project(rows, w, gate_w):
    cands, width = rows[0].shape
    split = len(rows)
    depth = split * width
    step = 256
    heads = width // DH
    block = pl.BlockSpec((step, width), lambda i: (i, 0))
    by_head = pl.BlockSpec((heads, step, DH), lambda i: (0, i, 0))
    whole = lambda a: pl.BlockSpec(a.shape, lambda i: (0, 0))
    return pl.pallas_call(
        project_kernel,
        out_shape=(
            jax.ShapeDtypeStruct((split, cands, width), jnp.bfloat16),
            pltpu.HBM((heads, cands, DH), jnp.bfloat16),
            pltpu.HBM((heads, cands, DH), jnp.float32),
        ),
        grid=(cands // step,),
        in_specs=[block] * split + [whole(w)] + [whole(g) for g in gate_w],
        out_specs=(
            pl.BlockSpec((split, step, width), lambda i: (0, i, 0)),
            by_head,
            by_head,
        ),
        scratch_shapes=[pltpu.VMEM((step, depth), jnp.bfloat16)],
        compiler_params=pltpu.CompilerParams(vmem_limit_bytes=VMEM),
        cost_estimate=cost(2 * cands * depth * 7 * width, 8 << 20, cands * 7 * width),
        name="project",
    )(*[hbm(r) for r in rows], hbm(w), *[hbm(g) for g in gate_w])


def attend_kernel(query, got, mask, own, *refs):
    out, weights, total = refs[-3:]
    step = pl.program_id(0)
    n = got.shape[0] * BLK
    keys = got[:, :BLK, :].reshape(n, DH)
    for g in range(weights.shape[0] // GROUP):
        rows = slice(g * GROUP, (g + 1) * GROUP)
        s = lax.dot_general(
            query[0, rows, :], keys, (((1,), (1,)), ((), ())), preferred_element_type=jnp.float32
        )
        weights[rows, :] = silu(s * mask[g : g + 1, :]).astype(jnp.bfloat16)
    part = jnp.dot(
        weights[...], got[:, BLK : 2 * BLK, :].reshape(n, DH), preferred_element_type=jnp.float32
    )

    @pl.when(step == 0)
    def _():
        total[...] = own[0] + part

    @pl.when(step > 0)
    def _():
        total[...] += part

    @pl.when(step == pl.num_programs(0) - 1)
    def _():
        done = total[...].astype(jnp.bfloat16)
        for i in range(out.shape[0]):
            out[i] = done


def attend(head, query, got, mask, own, copies, after=()):
    shards = got.shape[0]
    _, cands, _ = query.shape
    n = PER * BLK
    of_head = pl.BlockSpec((1, cands, DH), lambda i: (head, 0, 0))
    return pl.pallas_call(
        attend_kernel,
        out_shape=jax.ShapeDtypeStruct((copies, cands, DH), jnp.bfloat16),
        grid=(shards // PER,),
        in_specs=[
            of_head,
            pl.BlockSpec((PER, 2 * BLK, DH), lambda i: (i, 0, 0)),
            pl.BlockSpec((mask.shape[0], n), lambda i: (0, i)),
            of_head,
        ]
        + [pl.BlockSpec(memory_space=pl.ANY)] * len(after),
        out_specs=WHOLE,
        scratch_shapes=[
            pltpu.VMEM((cands, n), jnp.bfloat16),
            pltpu.VMEM((cands, DH), jnp.float32),
        ],
        compiler_params=pltpu.CompilerParams(vmem_limit_bytes=VMEM),
        cost_estimate=cost(4 * cands * shards * BLK * DH, 4 << 20, cands * shards * BLK),
        name="attend",
    )(hbm(query), hbm(got), hbm(mask), hbm(own), *after)


def finish_kernel(a0, a1, a2, a3, last, gates, w, rows, out, made, sems):
    split, cands, width = gates.shape
    total = split * width
    count = sems.shape[0]
    step = cands // count
    part = lax.axis_index("mp")
    place = [lax.rem(part + (split - d), split) for d in range(split)]
    stores = []
    for b in range(count):
        here = slice(b * step, (b + 1) * step)
        pieces = [
            jnp.concatenate([a[0, here, :], last[place[d], here, :]], axis=1).astype(jnp.float32)
            for d, a in enumerate((a0, a1, a2, a3))
        ]
        mean = jnp.sum(sum(pieces), axis=1, keepdims=True) / total
        centred = [p - mean for p in pieces]
        spread = jnp.sum(sum(c * c for c in centred), axis=1, keepdims=True) / total
        scale = lax.rsqrt(spread + EPS)
        result = rows[here, :].astype(jnp.float32)
        for d in range(split):
            gate = gates[place[d], here, :].astype(jnp.float32)
            result += jnp.dot(
                (centred[d] * scale * gate).astype(jnp.bfloat16),
                w[place[d]],
                preferred_element_type=jnp.float32,
            )
        made[here, :] = result.astype(made.dtype)
        at = pl.ds(b * step, step)
        stores.append(pltpu.make_async_copy(made.at[at], out.at[at], sems.at[b]))
        stores[-1].start()
    for store in stores:
        store.wait()


def finish(firsts, last, gates, w, rows):
    split, cands, width = gates.shape
    return pl.pallas_call(
        finish_kernel,
        out_shape=pltpu.HBM(rows.shape, jnp.bfloat16),
        in_specs=[WHOLE] * (len(firsts) + 4),
        out_specs=IN_HBM,
        scratch_shapes=[
            pltpu.VMEM(rows.shape, jnp.bfloat16),
            pltpu.SemaphoreType.DMA((4,)),
        ],
        compiler_params=pltpu.CompilerParams(vmem_limit_bytes=VMEM),
        cost_estimate=cost(2 * cands * split * width * rows.shape[1], 3 << 20),
        name="finish",
    )(*firsts, last, gates, w, rows)


def local(
    cand_feats, cand_perm, w_in, w_out, cache_k, cache_v, hist_len, hist_home, hist_slot, hist_mask
):
    shards = lax.axis_size("req")
    split = lax.axis_size("mp")
    me = lax.axis_index("req")
    part = lax.axis_index("mp")
    columns = cand_feats.shape[1]
    halves = columns // DH
    cand_slot = cand_feats.shape[0] // shards
    cands = cand_perm.shape[1]
    width = w_in.shape[2]

    def back(x, d):
        return lax.ppermute(x, "mp", [(i, (i + d) % split) for i in range(split)])

    exchange = functools.partial(
        lax.all_to_all, axis_name="req", split_axis=0, concat_axis=0, tiled=True
    )
    history = (hist_home, hist_slot, cache_k, cache_v)
    got_first = exchange(pack(0, *history, cand=cand_feats))

    w_gate = w_in[:, 0, :]
    gate_w = [back(w_gate, d) for d in range(1, split)]
    own_out = []
    for d in range(split):
        piece = lax.dynamic_slice_in_dim(w_out, (part + d) % split * columns, columns, axis=1)
        own_out.append(back(piece, d) if d else piece)
    backs = (part - jnp.arange(split, dtype=jnp.int32)) % split
    own_out = jnp.take(jnp.stack(own_out), backs, axis=0, mode="clip")

    home = hist_home[me]
    order = (jnp.arange(shards, dtype=jnp.int32) - home) % shards
    seen = jnp.take(hist_mask[0], order, axis=1, mode="clip").astype(jnp.float32)
    inside = order[:, None] * BLK + jnp.arange(BLK, dtype=jnp.int32)[None, :] < hist_len[0]
    mask = seen[:, :, None] * jnp.where(inside, 0.5 * DH**-0.5, 0.0)[None]
    mask = mask.reshape(hist_mask.shape[1], shards * BLK)

    w_flat = w_in.reshape(w_in.shape[0], 4 * width)
    ready = [*gate_w, own_out, mask, w_flat]
    got_second = exchange(pack(1, *history, after=ready))

    arrived = (
        got_first[:, 2 * BLK :, :]
        .reshape(shards, halves, cand_slot, DH)
        .transpose(0, 2, 1, 3)
        .reshape(cands, columns)
    )
    own_rows = jnp.take(arrived, cand_perm[0], axis=0, mode="clip")
    rows = [own_rows] + [back(own_rows, d) for d in range(1, split)]
    gates, query, own = project(rows, w_flat, gate_w)

    first = attend(0, query, got_first, mask, own, 1)
    firsts = [first] + [back(first, d) for d in range(1, split)]
    last = attend(1, query, got_second, mask, own, split, after=firsts[1:])
    last = lax.all_to_all(last, "mp", split_axis=0, concat_axis=0, tiled=True)
    return finish(firsts, last, gates, own_out, own_rows)


def solution(mesh):
    in_specs = (
        P("req", "mp"),
        P("req", None),
        P(None, None, "mp"),
        P("mp", None),
        P("req", None, "mp"),
        P("req", None, "mp"),
        P("req"),
        P(),
        P(),
        P("req", None, None),
    )
    out_specs = P("req", "mp")
    return jax.shard_map(local, mesh=mesh, in_specs=in_specs, out_specs=out_specs, check_vma=False)
```

```python
import functools

import jax
import jax.numpy as jnp
from jax import lax
from jax.experimental import pallas as pl
from jax.experimental.pallas import tpu as pltpu
from jax.sharding import PartitionSpec as P

HEADS = 8
DH = 128
BLK = 32
MAXBLK = 128
GROUP = 128
CSLOT = 4
PER = 64
EPS = 1e-05
VMEM = 28 * 1024 * 1024
WHOLE = pl.BlockSpec(memory_space=pltpu.VMEM)
IN_HBM = pl.BlockSpec(memory_space=pltpu.HBM)


def hbm(x):
    return pltpu.with_memory_space_constraint(x, pltpu.HBM)


def cost(flops, nbytes, trans=0):
    return pl.CostEstimate(flops=flops, bytes_accessed=nbytes, transcendentals=trans)


def spread_rows(rows_in):
    count, columns = rows_in.shape
    halves = columns // DH
    x = jnp.concatenate([rows_in[:, h * DH : (h + 1) * DH] for h in range(halves)], axis=0)
    shape = (halves * count, halves * count)
    at = lax.broadcasted_iota(jnp.int32, shape, 0)
    source = lax.broadcasted_iota(jnp.int32, shape, 1)
    group, inner = at // (CSLOT * halves), at % (CSLOT * halves)
    wanted = (inner // CSLOT) * count + group * CSLOT + inner % CSLOT
    pick = jnp.where(source == wanted, 1.0, 0.0).astype(jnp.bfloat16)
    return jnp.dot(pick, x, preferred_element_type=jnp.float32).astype(rows_in.dtype)


def pack_kernel(head, with_rows, home_in, table_in, keys_in, values_in, *refs):
    out, home, table, keys, values, cand, made, index_sem, load_sem, store_sem = refs[-10:]
    cols = pl.ds(head * DH, DH)
    pairs = [(home_in, home), (table_in, table)]
    if with_rows:
        pairs.append((refs[0], cand))
    indices = [pltpu.make_async_copy(a, b, index_sem.at[i]) for i, (a, b) in enumerate(pairs)]
    blocks = [
        pltpu.make_async_copy(a.at[:, :, cols], b, load_sem.at[i])
        for i, (a, b) in enumerate(((keys_in, keys), (values_in, values)))
    ]
    for load in [indices[1], indices[0], *indices[2:], *blocks]:
        load.start()
    shards, rows, _ = made.shape
    if with_rows:
        indices[2].wait()
        step = 32
        for b in range(0, cand.shape[0], step):
            x = spread_rows(cand[b : b + step, :])
            n = step // CSLOT
            made[b // CSLOT : b // CSLOT + n, 2 * BLK :, :] = x.reshape(n, rows - 2 * BLK, DH)
    for load in indices[:2] + blocks:
        load.wait()
    me = lax.axis_index("req")
    per = shards // store_sem.shape[0]
    stores = []
    for c in range(store_sem.shape[0]):
        chunk = pl.ds(c * per, per)
        for r in range(c * per, (c + 1) * per):
            behind = me - home[r]
            slot = table[r, jnp.where(behind < 0, behind + shards, behind)]
            made[r, :BLK, :] = keys[slot]
            made[r, BLK : 2 * BLK, :] = values[slot]
        stores.append(pltpu.make_async_copy(made.at[chunk], out.at[chunk], store_sem.at[c]))
        stores[-1].start()
    for store in stores:
        store.wait()


def pack(head, home, table, keys, values, cand=None, after=()):
    shards = home.shape[0]
    rows = 2 * BLK
    args = [hbm(home), hbm(table), hbm(keys), hbm(values)]
    held_cand = (16, DH)
    if cand is not None:
        rows += cand.shape[0] * cand.shape[1] // (DH * shards)
        args.append(hbm(cand))
        held_cand = cand.shape
    out_shape = (shards, rows, DH)
    held = (keys.shape[0], BLK, DH)
    return pl.pallas_call(
        functools.partial(pack_kernel, head, cand is not None),
        out_shape=pltpu.HBM(out_shape, keys.dtype),
        in_specs=[IN_HBM] * len(args) + [pl.BlockSpec(memory_space=pl.ANY)] * len(after),
        out_specs=IN_HBM,
        scratch_shapes=[
            pltpu.SMEM(home.shape, jnp.int32),
            pltpu.SMEM(table.shape, jnp.int32),
            pltpu.VMEM(held, keys.dtype),
            pltpu.VMEM(held, keys.dtype),
            pltpu.VMEM(held_cand, keys.dtype),
            pltpu.VMEM(out_shape, keys.dtype),
            pltpu.SemaphoreType.DMA((3,)),
            pltpu.SemaphoreType.DMA((2,)),
            pltpu.SemaphoreType.DMA((8,)),
        ],
        compiler_params=pltpu.CompilerParams(vmem_limit_bytes=VMEM),
        cost_estimate=cost(0, 2 * shards * rows * DH * 2),
        name="pack",
    )(*args, *after)


def silu(half):
    return half + half * jnp.tanh(half)


def project_kernel(r0, r1, r2, r3, w, g1, g2, g3, gates, query, own, normed):
    pieces = [r[...].astype(jnp.float32) for r in (r0, r1, r2, r3)]
    split = len(pieces)
    width = r0.shape[1]
    total = split * width
    part = lax.axis_index("mp")
    place = [lax.rem(part + (split - d), split) for d in range(split)]
    mean = sum(jnp.sum(p, axis=1, keepdims=True) for p in pieces) / total
    centred = [p - mean for p in pieces]
    spread = sum(jnp.sum(c * c, axis=1, keepdims=True) for c in centred) / total
    scale = lax.rsqrt(spread + EPS)
    for d in range(split):
        at = pl.multiple_of(place[d] * width, width)
        normed[:, pl.ds(at, width)] = (centred[d] * scale).astype(jnp.bfloat16)
    x = normed[...]

    def times(matrix):
        return silu(0.5 * jnp.dot(x, matrix, preferred_element_type=jnp.float32)).astype(
            jnp.bfloat16
        )

    gates[place[0]] = times(w[:, :width])
    for d, g in ((1, g1), (2, g2), (3, g3)):
        gates[place[d]] = times(g[...])
    value = times(w[:, width : 2 * width]).astype(jnp.float32)
    q = times(w[:, 2 * width : 3 * width])
    key = times(w[:, 3 * width :]).astype(jnp.float32)
    product = q.astype(jnp.float32) * key
    for h in range(width // DH):
        cols = slice(h * DH, (h + 1) * DH)
        half = jnp.sum(product[:, cols], axis=1, keepdims=True) * (0.5 * DH**-0.5)
        own[h] = silu(half) * value[:, cols]
        query[h] = q[:, cols]


def project(rows, w, gate_w):
    cands, width = rows[0].shape
    split = len(rows)
    depth = split * width
    step = 256
    heads = width // DH
    block = pl.BlockSpec((step, width), lambda i: (i, 0))
    by_head = pl.BlockSpec((heads, step, DH), lambda i: (0, i, 0))
    whole = lambda a: pl.BlockSpec(a.shape, lambda i: (0, 0))
    return pl.pallas_call(
        project_kernel,
        out_shape=(
            jax.ShapeDtypeStruct((split, cands, width), jnp.bfloat16),
            pltpu.HBM((heads, cands, DH), jnp.bfloat16),
            pltpu.HBM((heads, cands, DH), jnp.float32),
        ),
        grid=(cands // step,),
        in_specs=[block] * split + [whole(w)] + [whole(g) for g in gate_w],
        out_specs=(
            pl.BlockSpec((split, step, width), lambda i: (0, i, 0)),
            by_head,
            by_head,
        ),
        scratch_shapes=[pltpu.VMEM((step, depth), jnp.bfloat16)],
        compiler_params=pltpu.CompilerParams(vmem_limit_bytes=VMEM),
        cost_estimate=cost(2 * cands * depth * 7 * width, 8 << 20, cands * 7 * width),
        name="project",
    )(*[hbm(r) for r in rows], hbm(w), *[hbm(g) for g in gate_w])


def attend_kernel(query, got, mask, own, *refs):
    out, weights, total = refs[-3:]
    step = pl.program_id(0)
    n = got.shape[0] * BLK
    keys = got[:, :BLK, :].reshape(n, DH)
    for g in range(weights.shape[0] // GROUP):
        rows = slice(g * GROUP, (g + 1) * GROUP)
        s = lax.dot_general(
            query[0, rows, :], keys, (((1,), (1,)), ((), ())), preferred_element_type=jnp.float32
        )
        weights[rows, :] = silu(s * mask[g : g + 1, :]).astype(jnp.bfloat16)
    part = jnp.dot(
        weights[...], got[:, BLK : 2 * BLK, :].reshape(n, DH), preferred_element_type=jnp.float32
    )

    @pl.when(step == 0)
    def _():
        total[...] = own[0] + part

    @pl.when(step > 0)
    def _():
        total[...] += part

    @pl.when(step == pl.num_programs(0) - 1)
    def _():
        done = total[...].astype(jnp.bfloat16)
        for i in range(out.shape[0]):
            out[i] = done


def attend(head, query, got, mask, own, copies, after=()):
    shards = got.shape[0]
    _, cands, _ = query.shape
    n = PER * BLK
    of_head = pl.BlockSpec((1, cands, DH), lambda i: (head, 0, 0))
    return pl.pallas_call(
        attend_kernel,
        out_shape=jax.ShapeDtypeStruct((copies, cands, DH), jnp.bfloat16),
        grid=(shards // PER,),
        in_specs=[
            of_head,
            pl.BlockSpec((PER, 2 * BLK, DH), lambda i: (i, 0, 0)),
            pl.BlockSpec((mask.shape[0], n), lambda i: (0, i)),
            of_head,
        ]
        + [pl.BlockSpec(memory_space=pl.ANY)] * len(after),
        out_specs=WHOLE,
        scratch_shapes=[
            pltpu.VMEM((cands, n), jnp.bfloat16),
            pltpu.VMEM((cands, DH), jnp.float32),
        ],
        compiler_params=pltpu.CompilerParams(vmem_limit_bytes=VMEM),
        cost_estimate=cost(4 * cands * shards * BLK * DH, 4 << 20, cands * shards * BLK),
        name="attend",
    )(hbm(query), hbm(got), hbm(mask), hbm(own), *after)


def finish_kernel(a0, a1, a2, a3, last, gates, w, rows, out, made, sems):
    split, cands, width = gates.shape
    total = split * width
    count = sems.shape[0]
    step = cands // count
    part = lax.axis_index("mp")
    place = [lax.rem(part + (split - d), split) for d in range(split)]
    stores = []
    for b in range(count):
        here = slice(b * step, (b + 1) * step)
        pieces = [
            jnp.concatenate([a[0, here, :], last[place[d], here, :]], axis=1).astype(jnp.float32)
            for d, a in enumerate((a0, a1, a2, a3))
        ]
        mean = jnp.sum(sum(pieces), axis=1, keepdims=True) / total
        centred = [p - mean for p in pieces]
        spread = jnp.sum(sum(c * c for c in centred), axis=1, keepdims=True) / total
        scale = lax.rsqrt(spread + EPS)
        result = rows[here, :].astype(jnp.float32)
        for d in range(split):
            gate = gates[place[d], here, :].astype(jnp.float32)
            result += jnp.dot(
                (centred[d] * scale * gate).astype(jnp.bfloat16),
                w[place[d]],
                preferred_element_type=jnp.float32,
            )
        made[here, :] = result.astype(made.dtype)
        at = pl.ds(b * step, step)
        stores.append(pltpu.make_async_copy(made.at[at], out.at[at], sems.at[b]))
        stores[-1].start()
    for store in stores:
        store.wait()


def finish(firsts, last, gates, w, rows):
    split, cands, width = gates.shape
    return pl.pallas_call(
        finish_kernel,
        out_shape=pltpu.HBM(rows.shape, jnp.bfloat16),
        in_specs=[WHOLE] * (len(firsts) + 4),
        out_specs=IN_HBM,
        scratch_shapes=[
            pltpu.VMEM(rows.shape, jnp.bfloat16),
            pltpu.SemaphoreType.DMA((4,)),
        ],
        compiler_params=pltpu.CompilerParams(vmem_limit_bytes=VMEM),
        cost_estimate=cost(2 * cands * split * width * rows.shape[1], 3 << 20),
        name="finish",
    )(*firsts, last, gates, w, rows)


def local(
    cand_feats, cand_perm, w_in, w_out, cache_k, cache_v, hist_len, hist_home, hist_slot, hist_mask
):
    shards = lax.axis_size("req")
    split = lax.axis_size("mp")
    me = lax.axis_index("req")
    part = lax.axis_index("mp")
    columns = cand_feats.shape[1]
    halves = columns // DH
    cand_slot = cand_feats.shape[0] // shards
    cands = cand_perm.shape[1]
    width = w_in.shape[2]

    def back(x, d):
        return lax.ppermute(x, "mp", [(i, (i + d) % split) for i in range(split)])

    exchange = functools.partial(
        lax.all_to_all, axis_name="req", split_axis=0, concat_axis=0, tiled=True
    )
    history = (hist_home, hist_slot, cache_k, cache_v)
    got_first = exchange(pack(0, *history, cand=cand_feats))

    w_gate = w_in[:, 0, :]
    gate_w = [back(w_gate, d) for d in range(1, split)]
    own_out = []
    for d in range(split):
        piece = lax.dynamic_slice_in_dim(w_out, (part + d) % split * columns, columns, axis=1)
        own_out.append(back(piece, d) if d else piece)
    backs = (part - jnp.arange(split, dtype=jnp.int32)) % split
    own_out = jnp.take(jnp.stack(own_out), backs, axis=0, mode="clip")

    home = hist_home[me]
    order = (jnp.arange(shards, dtype=jnp.int32) - home) % shards
    seen = jnp.take(hist_mask[0], order, axis=1, mode="clip").astype(jnp.float32)
    inside = order[:, None] * BLK + jnp.arange(BLK, dtype=jnp.int32)[None, :] < hist_len[0]
    mask = seen[:, :, None] * jnp.where(inside, 0.5 * DH**-0.5, 0.0)[None]
    mask = mask.reshape(hist_mask.shape[1], shards * BLK)

    w_flat = w_in.reshape(w_in.shape[0], 4 * width)
    ready = [*gate_w, own_out, mask, w_flat]
    got_second = exchange(pack(1, *history, after=ready))

    arrived = (
        got_first[:, 2 * BLK :, :]
        .reshape(shards, halves, cand_slot, DH)
        .transpose(0, 2, 1, 3)
        .reshape(cands, columns)
    )
    own_rows = jnp.take(arrived, cand_perm[0], axis=0, mode="clip")
    rows = [own_rows] + [back(own_rows, d) for d in range(1, split)]
    gates, query, own = project(rows, w_flat, gate_w)

    first = attend(0, query, got_first, mask, own, 1)
    firsts = [first] + [back(first, d) for d in range(1, split)]
    last = attend(1, query, got_second, mask, own, split, after=firsts[1:])
    last = lax.all_to_all(last, "mp", split_axis=0, concat_axis=0, tiled=True)
    return finish(firsts, last, gates, own_out, own_rows)


def solution(mesh):
    in_specs = (
        P("req", "mp"),
        P("req", None),
        P(None, None, "mp"),
        P("mp", None),
        P("req", None, "mp"),
        P("req", None, "mp"),
        P("req"),
        P(),
        P(),
        P("req", None, None),
    )
    out_specs = P("req", "mp")
    return jax.shard_map(local, mesh=mesh, in_specs=in_specs, out_specs=out_specs, check_vma=False)
```
